512 devices in a mesh: exp: 8 (over x, y_hi), tp: 64 (over y_lo, z, core).
Axes of the slice: x: 4, y: 8 (y_hi: 2, y_lo: 4; y = y_hi * 4 + y_lo), z: 8, core: 2. Of those that a mesh axis runs over, the one named last changes fastest.
Arguments:
- hidden_state: bfloat16 [1024, 6144], P('exp', 'tp')
- norm_gain: bfloat16 [6144], P('tp'), may hold values from 0.099609375 to 1.8984375
- routes: int32 [1024, 2], P('exp'), may hold values from 0 to 7, all different within a row; in each aligned block of 128 rows (0 to 127, 128 to 255, ...) at most 64 rows name the same one
- gates: float32 [1024, 2], P('exp'), may hold values from 0.2 to 1
- w_gate: bfloat16 [8, 6144, 8192], P('exp', None, 'tp'), may hold values from -0.078125 to 0.078125
- w_up: bfloat16 [8, 6144, 8192], P('exp', None, 'tp'), may hold values from -0.078125 to 0.078125
- w_down: bfloat16 [8, 8192, 6144], P('exp', None, 'tp'), may hold values from -0.0625 to 0.0625
Outputs:
- mixed: bfloat16 [1024, 6144], P('exp', 'tp')
The draws below stay inside these ranges and needn't reach their ends.
Inputs may be any that keep to these rules, and one draw needn't show every extreme that they name: `routes`: the two experts of a row differ. Among the rows of one index of exp, no expert is named by more than 64 rows, a bound that some block reaches.
All inputs are finite; a program needn't handle non-finite values.
Results may differ from the reference program's by a relative error of at most 0.0071.
Values may be sent and summed in bfloat16 or wider, within the bound.
No kernel may reach another device: no remote copies, remote signals or barrier semaphores. Data moves between devices by JAX's collectives and lax.ppermute only.
A program may use at most 64 MiB of HBM per device.

```python
import math
import jax
import jax.numpy as jnp
import numpy as np
from jax import lax

D = 6144
FF = 8192
ROW_DEV = 128
EXPERTS = 8
ROWS = 1024
CAP = 64
N_EXP = 8


def draw_hidden_state(key, part):
    key = jax.random.fold_in(key, 11)
    key_rows, key_cols, key_base = jax.random.split(key, 3)
    row_scale = jnp.exp(jax.random.uniform(key_rows, (ROWS, 1), jnp.float32) * math.log(10.0))
    col_scale = jnp.exp(jax.random.uniform(key_cols, (1, D), jnp.float32) * math.log(10.0))
    base = jax.random.normal(key_base, (ROWS, D), jnp.float32)
    return (base * row_scale * col_scale / 5.0).astype(jnp.bfloat16)


def shard_levels(key, extent, cuts, low, largest):
    level = 1.0
    for dim, blocks in cuts:
        heights = jax.random.uniform(jax.random.fold_in(jax.random.fold_in(key, 6), dim), (blocks,), jnp.float32, low / len(cuts), largest / len(cuts))
        level = level * jnp.repeat(jnp.exp(heights), extent[dim] // blocks).reshape((-1,) + (1,) * (len(extent) - 1 - dim))
    return level


def assign_block(rng, own, number, rows, amount, top, reach, slope):
    order = jax.random.permutation(rng, amount)
    crowded, usual = load_shares(amount, rows * top, reach, slope, True), load_shares(amount, rows * top, reach, slope, False)
    places = jnp.arange(amount)

    def named(lengths, offset_by):
        used = int((lengths > 0).sum())
        fixed = max(1, used // 4)
        moved = fixed + (places - fixed + offset_by * (used - fixed)) % max(1, amount - fixed)
        return jnp.zeros((amount,), jnp.int32).at[order[jnp.where(places < fixed, places, moved)]].set(jnp.asarray(lengths, jnp.int32))

    lengths = jnp.where(number % 4 == 0, named(crowded, number // 4), named(usual, number - number // 4 - 1))
    mixed = jax.random.permutation(jax.random.fold_in(own, 3), amount)
    giver, receiver = mixed[0:amount // 2 * 2:2], mixed[1:amount // 2 * 2:2]
    margin = jnp.minimum(lengths[giver] - 1, reach - lengths[receiver]) // 2
    margin = jnp.where((giver == order[0]) | (receiver == order[0]) | (lengths[receiver] == 0), 0, jnp.maximum(margin, 0))
    moved = jax.random.randint(jax.random.fold_in(own, 4), (amount // 2,), 0, 1 << 20) % (margin + 1)
    lengths = lengths.at[giver].add(-moved).at[receiver].add(moved)
    members = jnp.searchsorted(jnp.cumsum(lengths), jnp.arange(rows * top), side="right").astype(jnp.int32)
    listing = members.reshape(top, rows).T
    listing = listing[jax.random.permutation(jax.random.fold_in(own, 1), rows)]
    offset_by = jax.random.randint(jax.random.fold_in(own, 2), (rows, 1), 0, top)
    return jnp.take_along_axis(listing, (jnp.arange(top)[None, :] + offset_by) % top, axis=1)


def load_shares(amount, total, most, skew, full):
    loads = [(1 << 20) // math.isqrt(grade ** skew) + 1 for grade in range(1, amount + 1)]
    largest = most if full else min(most, max(-(-total // amount), total * loads[0] // sum(loads)))
    least = 1 if total - largest >= amount - 1 else 0
    counts, spare = [largest] + [least] * (amount - 1), total - largest - least * (amount - 1)
    while spare > 0:
        movable = [i for i in range(1, amount) if counts[i] < largest] or [i for i in range(1, amount) if counts[i] < most]
        mass, budget = sum([loads[i] for i in movable]), spare
        for i in movable:
            extra = min(most - counts[i], max(1, budget * loads[i] // mass), spare)
            counts[i] = counts[i] + extra
            spare = spare - extra
    return np.array(counts)


def bell_draw(rng, shape, spread, reach, pieces=(), held_as=jnp.bfloat16):
    factor_of = shard_levels(rng, shape, pieces, -0.22, 0.18) if pieces else 1.0
    drawn = jax.random.normal(rng, shape, jnp.float32) * spread * factor_of
    return jnp.minimum(jnp.maximum(drawn, -reach), reach).astype(held_as)


def setup_inputs(seed: int = 0) -> dict:
    key_list = jax.random.split(jax.random.key(seed), 8)
    hidden_state = draw_hidden_state(jax.random.fold_in(key_list[7], 71), 0)
    norm_gain = jnp.clip(1.0 + 0.18 * jax.random.normal(key_list[1], (D,), jnp.float32), 0.099609375, 1.8984375).astype(jnp.bfloat16)
    routes_keys = jax.random.split(jax.random.fold_in(key_list[2], 1), ROWS // ROW_DEV)
    routes_turns = jax.random.permutation(jax.random.fold_in(key_list[2], 3), ROWS // ROW_DEV)
    routes = jax.vmap(lambda own, number: assign_block(jax.random.fold_in(key_list[2], 2), own, number, ROW_DEV, EXPERTS, 2, CAP, 2))(routes_keys, routes_turns).reshape((ROWS, 2))
    gates = jnp.clip(0.2 + 0.8 * jax.random.uniform(key_list[3], (ROWS, 2), jnp.float32) ** shard_levels(key_list[3], (ROWS, 2), ((0, 8),), -0.2, 0.2), 0.2, 1.0)
    w_gate = bell_draw(key_list[4], (EXPERTS, D, FF), D ** -0.5, 0.078125, ((0, 8), (2, 64)))
    w_up = bell_draw(key_list[5], (EXPERTS, D, FF), D ** -0.5, 0.078125, ((0, 8), (2, 64)))
    w_down = bell_draw(key_list[6], (EXPERTS, FF, D), FF ** -0.5, 0.0625, ((0, 8), (2, 64)))
    return dict(hidden_state=hidden_state, norm_gain=norm_gain, routes=routes, gates=gates, w_gate=w_gate, w_up=w_up, w_down=w_down)


def block_slots(flat_routes, experts):
    onehot = (flat_routes[:, None] == jnp.arange(experts, dtype=jnp.int32)[None, :]).astype(jnp.int32)
    before = jnp.cumsum(onehot, axis=0) - onehot
    return lax.optimization_barrier(jnp.sum(before * onehot, axis=1)).astype(jnp.int32)

def reference(hidden_state, norm_gain, routes, gates, w_gate, w_up, w_down):
    values = hidden_state.astype(jnp.float32)
    inv_rms = lax.rsqrt(lax.optimization_barrier(jnp.mean(values * values, axis=1)) + 1e-05)
    normed = (values * inv_rms[:, None] * norm_gain.astype(jnp.float32)[None, :]).astype(jnp.bfloat16)
    blocked = routes.reshape(N_EXP, ROW_DEV * 2)
    slots = jax.vmap(lambda b: block_slots(b, EXPERTS))(blocked)
    source = jnp.arange(N_EXP, dtype=jnp.int32)[:, None]
    position = (source * CAP + slots).astype(jnp.int32)
    pair_index = jnp.arange(ROW_DEV * 2, dtype=jnp.int32)[None, :]
    row_ids = (source * ROW_DEV + pair_index // 2).astype(jnp.int32)
    table = jnp.full((EXPERTS, N_EXP * CAP), ROWS, jnp.int32)
    table = table.at[blocked.reshape(-1), position.reshape(-1)].set(row_ids.reshape(-1))
    padded = jnp.concatenate([normed, jnp.zeros((1, D), jnp.bfloat16)], axis=0)

    def run_expert(expert):
        inputs = padded[table[expert]]
        gate = jnp.dot(inputs, w_gate[expert], preferred_element_type=jnp.float32)
        up = jnp.dot(inputs, w_up[expert], preferred_element_type=jnp.float32)
        act = (jax.nn.silu(gate) * up).astype(jnp.bfloat16)
        return jnp.dot(act, w_down[expert], preferred_element_type=jnp.float32).astype(jnp.bfloat16)
    outputs = lax.map(run_expert, jnp.arange(EXPERTS, dtype=jnp.int32))
    picked = outputs[routes, position.reshape(ROWS, 2)].astype(jnp.float32)
    mixed = lax.optimization_barrier(jnp.sum(gates[:, :, None] * picked, axis=1))
    return mixed.astype(jnp.bfloat16)
```

```python
import jax
import jax.numpy as jnp
from jax import lax
from jax.sharding import Mesh, PartitionSpec as P

D = 6144
EXPERTS = 8
NX, NYH, NYL, NZ, NC = 4, 2, 4, 8, 2
NZC = NZ * NC
ROW_DEV = 128
CAP = 64
EXTRA = 16
BF = jnp.bfloat16
F32 = jnp.float32


def three_parts(value):
    hi = value.astype(BF)
    rest = value - hi.astype(F32)
    mid = rest.astype(BF)
    lo = (rest - mid.astype(F32)).astype(BF)
    return [hi, mid, lo]


def from_parts(parts):
    parts = parts.astype(F32)
    return parts[0] + parts[1] + parts[2]


def slot_targets(route_rows, half):
    experts = jnp.arange(EXPERTS, dtype=jnp.int32)
    named = route_rows[:, :, None, :] == experts[None, None, :, None]
    mask = (named[0] | named[1]).astype(BF)
    earlier = lax.broadcasted_iota(jnp.int32, (ROW_DEV, ROW_DEV), 0) < lax.broadcasted_iota(
        jnp.int32, (ROW_DEV, ROW_DEV), 1
    )
    before = jnp.dot(
        mask.reshape(NYH * EXPERTS, ROW_DEV), earlier.astype(BF), preferred_element_type=F32
    ).reshape(1, NYH, EXPERTS, ROW_DEV)
    rank = jnp.sum(jnp.where(named, before, 0.0), axis=2).astype(jnp.int32)
    block = jnp.arange(NYH, dtype=jnp.int32)[None, :, None]
    target = (route_rows // 2) * (NYH * CAP) + block * CAP + rank
    return jnp.where(route_rows % 2 == half, target, -1).reshape(2, NYH * ROW_DEV)


def per_device(hidden_state, norm_gain, routes, gates, w_gate, w_up, w_down):
    half = lax.axis_index("yh")
    quarter = lax.axis_index("yl")

    values = hidden_state.astype(F32)
    scaled = (values * norm_gain.astype(F32)[None, :]).astype(BF).T
    extras = three_parts(jnp.sum(values * values, axis=1))
    extras += [routes[:, 0].astype(BF), routes[:, 1].astype(BF)]
    extras += three_parts(gates[:, 0]) + three_parts(gates[:, 1])
    extras += [jnp.zeros((ROW_DEV,), BF)] * (EXTRA - len(extras))
    payload = jnp.concatenate([scaled, jnp.stack(extras)], axis=0)

    with jax.named_scope("rows_over_y"):
        held = lax.all_gather(payload, ("yh", "yl"), axis=0, tiled=False)
    feats = held.shape[1] - EXTRA
    held = held.reshape(NYH, NYL, feats + EXTRA, ROW_DEV)
    info = held[:, 0, feats:, :]
    squares = jnp.sum(
        held[:, :, feats, :].astype(F32)
        + held[:, :, feats + 1, :].astype(F32)
        + held[:, :, feats + 2, :].astype(F32),
        axis=1,
    ).reshape(NYH * ROW_DEV)
    route_rows = info[:, 3:5, :].astype(jnp.int32).transpose(1, 0, 2)
    gate0 = from_parts(info[:, 5:8, :].transpose(1, 0, 2)).reshape(1, NYH * ROW_DEV)
    gate1 = from_parts(info[:, 8:11, :].transpose(1, 0, 2)).reshape(1, NYH * ROW_DEV)
    targets = slot_targets(route_rows, half)
    slot_ids = lax.broadcasted_iota(jnp.int32, (NX * NYH * CAP, NYH * ROW_DEV), 0)
    place0 = (slot_ids == targets[0][None, :]).astype(BF)
    place1 = (slot_ids == targets[1][None, :]).astype(BF)

    rows = held[:, :, :feats, :].transpose(1, 2, 0, 3).reshape(NYL * feats, NYH * ROW_DEV)
    square_rows = jnp.stack(three_parts(squares) + [jnp.zeros_like(squares, BF)] * (EXTRA - 3))
    rows = jnp.concatenate([rows, square_rows], axis=0)
    depth = rows.shape[0]
    outgoing = lax.dot_general(
        rows, place0 + place1, (((1,), (1,)), ((), ())), preferred_element_type=F32
    ).astype(BF)
    outgoing = outgoing.reshape(depth, NX, NYH * CAP).transpose(1, 0, 2)
    with jax.named_scope("rows_over_x"):
        incoming = lax.all_to_all(outgoing, "x", split_axis=0, concat_axis=0, tiled=True)
    slots = NX * NYH * CAP
    incoming = incoming.transpose(1, 0, 2).reshape(depth, slots)

    incoming, down, gate_cols, up_cols = lax.optimization_barrier(
        (incoming, w_down[0], w_gate[0], w_up[0])
    )
    with jax.named_scope("features_over_zc"):
        features = lax.all_gather(incoming, ("z", "c"), axis=0, tiled=True)
    units = down.shape[0] // NYL
    down_t = down.T.reshape(feats, NYL, units).transpose(1, 0, 2)
    pieces = [lax.dynamic_index_in_dim(down_t, quarter, 0, keepdims=False)]
    for m in range(1, NYL):
        piece = lax.dynamic_index_in_dim(down_t, quarter ^ m, 0, keepdims=False)
        with jax.named_scope("down_over_y"):
            pieces.append(lax.ppermute(piece, "yl", [(i, i ^ m) for i in range(NYL)]))
    pieces = jnp.stack(pieces)
    down_part = jnp.concatenate(
        [lax.dynamic_index_in_dim(pieces, quarter ^ j, 0, keepdims=False) for j in range(NYL)], axis=0
    )

    def reordered(cols):
        cols = cols.reshape(NYL, NZC, feats, cols.shape[1]).transpose(1, 0, 2, 3)
        cols = cols.reshape(NZC, NYL * feats, cols.shape[3])
        return jnp.pad(cols, ((0, 0), (0, EXTRA), (0, 0)))

    both = jnp.concatenate([reordered(gate_cols), reordered(up_cols)], axis=2)
    both = both.reshape(NZC * depth, both.shape[2])
    squares = features.reshape(NZC, depth, slots)[:, NYL * feats : NYL * feats + 3, :]
    inv_rms = lax.rsqrt(jnp.sum(squares.astype(F32), axis=(0, 1)) / D + 1e-05)[None, :]
    hidden = lax.dot_general(both, features, (((0,), (0,)), ((), ())), preferred_element_type=F32)
    own = hidden.shape[0] // 2
    act = (jax.nn.silu(hidden[:own] * inv_rms) * (hidden[own:] * inv_rms)).astype(BF)

    with jax.named_scope("units_over_zc"):
        acts = lax.all_gather(act, ("z", "c"), axis=0, tiled=True)
    out = jnp.dot(down_part, acts, preferred_element_type=F32).astype(BF)
    out = out.reshape(NYL * feats, NX, NYH * CAP).transpose(1, 0, 2)
    with jax.named_scope("out_over_x"):
        back = lax.all_to_all(out, "x", split_axis=0, concat_axis=0, tiled=True)
    back = back.transpose(1, 0, 2).reshape(NYL * feats, slots)
    mixed = gate0 * jnp.dot(back, place0, preferred_element_type=F32) + gate1 * jnp.dot(
        back, place1, preferred_element_type=F32
    )
    mixed = mixed.reshape(NYL, feats, NYH, ROW_DEV).transpose(2, 0, 1, 3)
    mixed = mixed.reshape(NYH * NYL, feats, ROW_DEV).astype(BF)
    with jax.named_scope("out_over_y"):
        parts = lax.all_to_all(mixed, ("yh", "yl"), split_axis=0, concat_axis=0, tiled=True)
    return jnp.sum(parts.astype(F32), axis=0).T.astype(BF)


def solution(mesh):
    fine = Mesh(mesh.devices.reshape(NX, NYH, NYL, NZ, NC), ("x", "yh", "yl", "z", "c"))
    exp, tp = ("x", "yh"), ("yl", "z", "c")
    in_specs = (
        P(exp, tp),
        P(tp),
        P(exp, None),
        P(exp, None),
        P(exp, None, tp),
        P(exp, None, tp),
        P(exp, None, tp),
    )
    return jax.shard_map(
        per_device, mesh=fine, in_specs=in_specs, out_specs=P(exp, tp), check_vma=False
    )
```

```python
import functools

import jax
import jax.numpy as jnp
from jax import lax
from jax.experimental import pallas as pl
from jax.experimental.pallas import tpu as pltpu
from jax.sharding import Mesh, PartitionSpec as P

D = 6144
EXPERTS = 8
NX, NYH, NYL, NZ, NC = 4, 2, 4, 8, 2
NZC = NZ * NC
FEATS = 96
ROW_DEV = 128
CAP = 64
SLOTS = EXPERTS * CAP
EXTRA = 16
DEPTH = NYL * FEATS + EXTRA
KSTEPS = 5
BF = jnp.bfloat16
F32 = jnp.float32
I32 = jnp.int32
BIG = 3.0e38
NT = (((1,), (1,)), ((), ()))
TN = (((0,), (0,)), ((), ()))
VMEM_LIMIT = 40 * 1024 * 1024


def iota(shape, dim):
    return lax.broadcasted_iota(I32, shape, dim)


def one_hot(condition):
    return jnp.where(condition, 1.0, 0.0).astype(BF)


def dot(a, b, dims=(((1,), (0,)), ((), ()))):
    return lax.dot_general(a, b, dims, preferred_element_type=F32)


def call(body, out_shape, *args, flops=1_000_000, moved=1_000_000, scalars=0, **kw):
    specs = [pl.BlockSpec(memory_space=pltpu.SMEM)] * scalars
    specs += [pl.BlockSpec(memory_space=pltpu.VMEM)] * (len(args) - scalars)
    return pl.pallas_call(
        body,
        out_shape=out_shape,
        in_specs=specs,
        out_specs=jax.tree.map(lambda _: pl.BlockSpec(memory_space=pltpu.VMEM), out_shape),
        compiler_params=pltpu.CompilerParams(vmem_limit_bytes=VMEM_LIMIT),
        cost_estimate=pl.CostEstimate(flops=flops, bytes_accessed=moved, transcendentals=0),
        **kw,
    )(*args)


def dispatch_body(hidden_ref, gain_ref, routes_ref, out_ref, target_ref):
    diagonal = iota((FEATS, FEATS), 0) == iota((FEATS, FEATS), 1)
    gain = jnp.sum(jnp.where(diagonal, gain_ref[...].astype(F32), 0.0), axis=1, keepdims=True)
    values = hidden_ref[...].astype(F32)
    scaled = jnp.clip(values * gain, -BIG, BIG)
    squares = jnp.minimum(jnp.sum(values * values, axis=0, keepdims=True), BIG)
    hi = squares.astype(BF).astype(F32)
    mid = (squares - hi).astype(BF).astype(F32)
    low = squares - hi - mid
    row = iota((ROW_DEV - FEATS, ROW_DEV), 0)
    parts = jnp.where(row == 0, hi, jnp.where(row == 1, mid, jnp.where(row == 2, low, 0.0)))
    rows = jnp.concatenate([scaled, parts], axis=0).astype(BF)

    first, second = routes_ref[0:1, :], routes_ref[1:2, :]
    expert = iota((2 * EXPERTS, ROW_DEV), 0)
    named0, named1 = expert == first, expert == second
    earlier = one_hot(iota((ROW_DEV, ROW_DEV), 0) < iota((ROW_DEV, ROW_DEV), 1))
    before = dot(one_hot(named0 | named1), earlier)
    rank0 = jnp.sum(jnp.where(named0, before, 0.0), axis=0, keepdims=True).astype(I32)
    rank1 = jnp.sum(jnp.where(named1, before, 0.0), axis=0, keepdims=True).astype(I32)
    target0, target1 = first * CAP + rank0, second * CAP + rank1
    target_ref[...] = jnp.where(iota((8, ROW_DEV), 0) == 0, target0, target1)
    slot = iota((SLOTS, ROW_DEV), 0)
    place = one_hot((slot == target0) | (slot == target1))
    sent = dot(place, rows, NT).astype(BF).reshape(EXPERTS, CAP, ROW_DEV)
    for j in range(NYL):
        out_ref[:, j] = sent


def turn_body(in_ref, out_ref):
    eye = one_hot(iota((FEATS, ROW_DEV), 0) == iota((FEATS, ROW_DEV), 1))
    row, lane = iota((EXTRA, ROW_DEV), 0), iota((EXTRA, ROW_DEV), 1)
    extra = jnp.zeros((EXTRA, SLOTS), F32)
    for j in range(NYL):
        rows = in_ref[:, j].reshape(SLOTS, ROW_DEV)
        out_ref[j * FEATS : (j + 1) * FEATS, :] = dot(eye, rows, NT).astype(BF)
        pick = one_hot((row - 3 * j == lane - FEATS) & (row >= 3 * j) & (row < 3 * j + 3))
        extra += dot(pick, rows, NT)
    out_ref[NYL * FEATS :, :] = extra.astype(BF)


def act_body(w_ref, x_ref, *rest):
    out_ref, acc_ref = rest[-2:]
    step = pl.program_id(0)

    @pl.when(step == 0)
    def _():
        acc_ref[...] = jnp.zeros_like(acc_ref)

    acc_ref[...] += dot(w_ref[...], x_ref[...])

    @pl.when(step == KSTEPS - 1)
    def _():
        units = out_ref.shape[1]
        inv_rms = lax.rsqrt(acc_ref[2 * units : 2 * units + 1, :] / D + 1e-05)
        gate = acc_ref[:units, :] * inv_rms
        up = acc_ref[units : 2 * units, :] * inv_rms
        act = (gate / (1.0 + jnp.exp(-gate)) * up).astype(BF)
        for z in range(NZ):
            out_ref[z] = act


def act_call(w, x, after):
    units = (w.shape[0] - EXTRA) // 2
    chunk = x.shape[0] // KSTEPS
    return pl.pallas_call(
        act_body,
        out_shape=jax.ShapeDtypeStruct((NZ, units, SLOTS), BF),
        grid=(KSTEPS,),
        in_specs=[
            pl.BlockSpec((w.shape[0], chunk), lambda k: (0, k)),
            pl.BlockSpec((chunk, SLOTS), lambda k: (k, 0)),
        ]
        + [pl.BlockSpec(memory_space=pl.ANY)] * len(after),
        out_specs=pl.BlockSpec((NZ, units, SLOTS), lambda k: (0, 0, 0)),
        scratch_shapes=[pltpu.VMEM((w.shape[0], SLOTS), F32)],
        compiler_params=pltpu.CompilerParams(
            dimension_semantics=("arbitrary",), vmem_limit_bytes=60 * 1024 * 1024
        ),
        cost_estimate=pl.CostEstimate(
            flops=2 * w.shape[0] * x.shape[0] * SLOTS, bytes_accessed=10_000_000, transcendentals=0
        ),
    )(w, x, *after)


def own_half_body(w_ref, x_ref, out_ref):
    out_ref[...] = dot(w_ref[...], x_ref[...])


def other_half_body(w_ref, x_ref, part_ref, out_ref):
    half = FEATS // 2
    out = part_ref[...] + dot(w_ref[...], x_ref[...])
    low = iota((half, 2 * CAP), 1) < CAP
    for j in range(NYL):
        for t in range(EXPERTS // 2):
            cols = slice(t * 2 * CAP, (t + 1) * 2 * CAP)
            a = out[j * FEATS : j * FEATS + half, cols]
            b = out[j * FEATS + half : (j + 1) * FEATS, cols]
            out_ref[2 * t, j] = jnp.where(low, a, pltpu.roll(b, CAP, 1)).astype(BF)
            out_ref[2 * t + 1, j] = jnp.where(low, pltpu.roll(a, CAP, 1), b).astype(BF)


def combine_body(in_ref, target_ref, gates_ref, out_ref):
    half = FEATS // 2
    target = jnp.concatenate([target_ref[0:1, :], target_ref[1:2, :]], axis=1)
    slot = iota((2 * CAP, 2 * ROW_DEV), 0) % CAP
    low = iota((half, 2 * CAP), 1) < CAP
    picked = jnp.zeros((FEATS, 2 * ROW_DEV), F32)
    for e in range(EXPERTS):
        place = one_hot(target - e * CAP == slot)
        total = in_ref[e, 0].astype(F32)
        for j in range(1, NYL):
            total += in_ref[e, j].astype(F32)
        total = jnp.concatenate([jnp.where(low, total, 0.0), jnp.where(low, 0.0, total)], axis=0)
        hi = total.astype(BF)
        rest = (total - hi.astype(F32)).astype(BF)
        picked += dot(hi, place) + dot(rest, place)
    mixed = gates_ref[0:1, :] * picked[:, :ROW_DEV] + gates_ref[1:2, :] * picked[:, ROW_DEV:]
    out_ref[...] = mixed.astype(BF)


def cut_body(place_ref, in_ref, *out_refs):
    width = out_refs[0].shape[1]
    for m, out_ref in enumerate(out_refs):
        start = pl.multiple_of(place_ref[m] * width, width)
        out_ref[...] = in_ref[:, pl.ds(start, width)]


def join_body(place_ref, *refs):
    pieces, (own_ref, other_ref) = refs[:NYL], refs[NYL:]
    step = pieces[0].shape[1] // NZC
    core = place_ref[NYL]
    for m, piece in enumerate(pieces):
        rows = pl.ds(pl.multiple_of(place_ref[m] * FEATS, FEATS), FEATS)
        for z in range(NZ):
            own = pl.ds(pl.multiple_of((2 * z + core) * step, step), step)
            other = pl.ds(pl.multiple_of((2 * z + 1 - core) * step, step), step)
            own_ref[rows, z * step : (z + 1) * step] = piece[:, own]
            other_ref[rows, z * step : (z + 1) * step] = piece[:, other]


def per_device(hidden_state, norm_gain, routes, gates, w_gate, w_up, w_down):
    quarter = lax.axis_index("yl")
    core = lax.axis_index("c")
    owners = ("x", "yh", "yl")

    outgoing, targets = call(
        dispatch_body,
        (
            jax.ShapeDtypeStruct((EXPERTS, NYL, CAP, ROW_DEV), BF),
            jax.ShapeDtypeStruct((8, ROW_DEV), I32),
        ),
        hidden_state.T,
        norm_gain[None, :],
        routes.T,
    )
    with jax.named_scope("rows_over_xy"):
        incoming = lax.all_to_all(
            outgoing.reshape(EXPERTS * NYL, CAP, ROW_DEV), owners, split_axis=0, concat_axis=0, tiled=True
        )
    incoming = incoming.reshape(EXPERTS, NYL, CAP, ROW_DEV)
    block = call(turn_body, jax.ShapeDtypeStruct((DEPTH, SLOTS), BF), incoming)

    block, down, gate_cols, up_cols = lax.optimization_barrier(
        (block, w_down[0], w_gate[0], w_up[0])
    )
    with jax.named_scope("features_over_zc"):
        features = lax.all_gather(block, ("z", "c"), axis=0, tiled=True)
    units = down.shape[0] // NYL
    places = jnp.stack([quarter ^ m for m in range(NYL)] + [core]).astype(I32)
    piece = jax.ShapeDtypeStruct((FEATS, units), BF)
    pieces = list(call(cut_body, (piece,) * NYL, places, down.T, scalars=1))
    for m in range(1, NYL):
        with jax.named_scope("down_over_y"):
            pieces[m] = lax.ppermute(pieces[m], "yl", [(i, i ^ m) for i in range(NYL)])
    part = jax.ShapeDtypeStruct((NYL * FEATS, units // NC), BF)
    down_own, down_other = call(join_body, (part, part), places, *pieces, scalars=1)

    def in_order(cols):
        cols = cols.reshape(NYL, NZC, FEATS, cols.shape[1]).transpose(1, 0, 2, 3)
        cols = cols.reshape(NZC, NYL * FEATS, cols.shape[3])
        return jnp.pad(cols, ((0, 0), (0, EXTRA), (0, 0)))

    is_part = (jnp.arange(DEPTH) >= NYL * FEATS) & (jnp.arange(DEPTH) < NYL * FEATS + 3 * NYL)
    count = jnp.broadcast_to(is_part.astype(BF)[None, :, None], (NZC, DEPTH, EXTRA))
    both = jnp.concatenate([in_order(gate_cols), in_order(up_cols), count], axis=2)
    both = both.reshape(NZC * DEPTH, both.shape[2]).T
    acts = act_call(both, features, (down_own, down_other))

    with jax.named_scope("units_over_z"):
        acts = lax.all_to_all(acts, "z", split_axis=0, concat_axis=0, tiled=True)
    acts = acts.reshape(units // NC, SLOTS)
    with jax.named_scope("units_over_c"):
        acts_other = lax.ppermute(acts, "c", [(0, 1), (1, 0)])
    part = call(
        own_half_body,
        jax.ShapeDtypeStruct((NYL * FEATS, SLOTS), F32),
        down_own,
        acts,
        flops=2 * NYL * FEATS * SLOTS * units // NC,
        moved=3_000_000,
    )
    out = call(
        other_half_body,
        jax.ShapeDtypeStruct((EXPERTS, NYL, FEATS // 2, 2 * CAP), BF),
        down_other,
        acts_other,
        part,
    )
    with jax.named_scope("out_over_xy"):
        back = lax.all_to_all(
            out.reshape(EXPERTS * NYL, FEATS // 2, 2 * CAP), owners, split_axis=0, concat_axis=0, tiled=True
        )
    back = back.reshape(EXPERTS, NYL, FEATS // 2, 2 * CAP)
    return call(
        combine_body, jax.ShapeDtypeStruct((FEATS, ROW_DEV), BF), back, targets, gates.T
    ).T


def solution(mesh):
    fine = Mesh(mesh.devices.reshape(NX, NYH, NYL, NZ, NC), ("x", "yh", "yl", "z", "c"))
    exp, tp = ("x", "yh"), ("yl", "z", "c")
    in_specs = (
        P(exp, tp),
        P(tp),
        P(exp, None),
        P(exp, None),
        P(exp, None, tp),
        P(exp, None, tp),
        P(exp, None, tp),
    )
    return jax.shard_map(
        per_device, mesh=fine, in_specs=in_specs, out_specs=P(exp, tp), check_vma=False
    )
```

```python
import functools

import jax
import jax.numpy as jnp
from jax import lax
from jax.experimental import pallas as pl
from jax.experimental.pallas import tpu as pltpu
from jax.sharding import Mesh, PartitionSpec as P

D = 6144
EXPERTS = 8
NX, NYH, NYA, NYB, NZ, NC = 4, 2, 2, 2, 8, 2
NYL = NYA * NYB
NZC = NZ * NC
FEATS = 96
GROUP = NYA * NC
ROW_DEV = 128
CAP = 64
PIECE = CAP // NC
SLOTS = EXPERTS * PIECE
EXTRA = 16
TILES = GROUP * FEATS // 128
PARTS = SLOTS // 128 * EXTRA
DEPTH = TILES * SLOTS + PARTS
PACK = 128 // PIECE
BF = jnp.bfloat16
F32 = jnp.float32
I32 = jnp.int32
BIG = 3.0e38
NT = (((1,), (1,)), ((), ()))
VMEM_LIMIT = 40 * 1024 * 1024


def iota(shape, dim):
    return lax.broadcasted_iota(I32, shape, dim)


def one_hot(condition):
    return jnp.where(condition, 1.0, 0.0).astype(BF)


def dot(a, b, dims=(((1,), (0,)), ((), ()))):
    return lax.dot_general(a, b, dims, preferred_element_type=F32)


def call(body, out_shape, *args, flops=1_000_000, moved=1_000_000, scalars=0, after=(), **kw):
    specs = [pl.BlockSpec(memory_space=pltpu.SMEM)] * scalars
    specs += [pl.BlockSpec(memory_space=pltpu.VMEM)] * (len(args) - scalars)
    specs += [pl.BlockSpec(memory_space=pl.ANY)] * len(after)
    return pl.pallas_call(
        body,
        out_shape=out_shape,
        in_specs=specs,
        out_specs=jax.tree.map(lambda _: pl.BlockSpec(memory_space=pltpu.VMEM), out_shape),
        compiler_params=pltpu.CompilerParams(vmem_limit_bytes=VMEM_LIMIT),
        cost_estimate=pl.CostEstimate(flops=flops, bytes_accessed=moved, transcendentals=0),
        **kw,
    )(*args, *after)


def dispatch_body(hidden_ref, gain_ref, routes_ref, out_ref, target_ref):
    diagonal = iota((FEATS, FEATS), 0) == iota((FEATS, FEATS), 1)
    gain = jnp.sum(jnp.where(diagonal, gain_ref[...].astype(F32), 0.0), axis=1, keepdims=True)
    values = hidden_ref[...].astype(F32)
    scaled = jnp.clip(values * gain, -BIG, BIG)
    squares = jnp.minimum(jnp.sum(values * values, axis=0, keepdims=True), BIG)
    hi = squares.astype(BF).astype(F32)
    mid = (squares - hi).astype(BF).astype(F32)
    low = squares - hi - mid
    row = iota((ROW_DEV - FEATS, ROW_DEV), 0)
    parts = jnp.where(row == 0, hi, jnp.where(row == 1, mid, jnp.where(row == 2, low, 0.0)))
    rows = jnp.concatenate([scaled, parts], axis=0).astype(BF)

    first, second = routes_ref[0:1, :], routes_ref[1:2, :]
    expert = iota((2 * EXPERTS, ROW_DEV), 0)
    named0, named1 = expert == first, expert == second
    earlier = one_hot(iota((ROW_DEV, ROW_DEV), 0) < iota((ROW_DEV, ROW_DEV), 1))
    before = dot(one_hot(named0 | named1), earlier)
    rank0 = jnp.sum(jnp.where(named0, before, 0.0), axis=0, keepdims=True).astype(I32)
    rank1 = jnp.sum(jnp.where(named1, before, 0.0), axis=0, keepdims=True).astype(I32)
    target0, target1 = first * CAP + rank0, second * CAP + rank1
    target_ref[...] = jnp.where(iota((8, ROW_DEV), 0) == 0, target0, target1)
    slot = iota((EXPERTS * CAP, ROW_DEV), 0)
    place = one_hot((slot == target0) | (slot == target1))
    sent = dot(place, rows, NT).astype(BF).reshape(EXPERTS, NC, PIECE, ROW_DEV)
    for j in range(NYA):
        out_ref[:, j] = sent


def turn_body(in_ref, out_ref, turned_ref):
    row, lane = iota((EXTRA, ROW_DEV), 0), iota((EXTRA, ROW_DEV), 1)
    source, column = iota((ROW_DEV, ROW_DEV), 0), iota((ROW_DEV, ROW_DEV), 1)
    extra = jnp.zeros((EXTRA, SLOTS), F32)
    rows = [in_ref[:, j].reshape(SLOTS, ROW_DEV) for j in range(GROUP)]
    for t in range(TILES):
        tile = jnp.zeros((SLOTS, ROW_DEV), F32)
        for j in range(GROUP):
            shift = t * ROW_DEV - j * FEATS
            if -ROW_DEV < shift < FEATS:
                pick = one_hot((source - column == shift) & (source < FEATS))
                tile += dot(rows[j], pick)
        turned_ref[t * SLOTS : (t + 1) * SLOTS, :] = tile.astype(BF)
    for j in range(GROUP):
        pick = one_hot((row - 3 * j == lane - FEATS) & (row >= 3 * j) & (row < 3 * j + 3))
        extra += dot(pick, rows[j], NT)
    for t in range(SLOTS // 128):
        start = TILES * SLOTS + t * EXTRA
        turned_ref[start : start + EXTRA, :] = extra[:, t * 128 : (t + 1) * 128].astype(BF)
    for z in range(NZ):
        out_ref[z] = turned_ref[...]


def halves_body(place_ref, gate_ref, up_ref, own_ref, other_ref):
    parity = place_ref[NYL + 1]
    for i, ref in enumerate((gate_ref, up_ref)):
        for j in range(NYA):
            own_ref[i, j] = ref[j, parity]
            other_ref[i, j] = ref[j, 1 - parity]


def products(x_ref, weight_refs, acc_ref):
    for z in range(0, NZ, 2):
        tiles, columns = [], []
        for i in range(z, z + 2):
            tiles += [x_ref[i, t * SLOTS : (t + 1) * SLOTS, :] for t in range(TILES)]
            weights = [w[k, :, i].reshape(GROUP * FEATS, 128) for w in weight_refs for k in range(2)]
            columns.append(jnp.concatenate(weights, axis=1))
        total = dot(jnp.concatenate(tiles, axis=1), jnp.concatenate(columns, axis=0))
        if z == 0:
            acc_ref[...] = total
        else:
            acc_ref[...] += total


def sums_of_squares(x_ref):
    parts = jnp.zeros((PARTS, 128), F32)
    for z in range(NZ):
        parts += x_ref[z, TILES * SLOTS :, :].astype(F32)
    sums = [
        jnp.sum(parts[t * EXTRA : (t + 1) * EXTRA], axis=0, keepdims=True) for t in range(SLOTS // 128)
    ]
    return jnp.concatenate(sums, axis=1)


def neighbour_body(w_ref, w2_ref, x_ref, out_ref, acc_ref):
    products(x_ref, (w_ref, w2_ref), acc_ref)
    out_ref[:SLOTS, :] = acc_ref[...].astype(BF)
    squares = jnp.minimum(sums_of_squares(x_ref), BIG)
    hi = squares.astype(BF).astype(F32)
    mid = (squares - hi).astype(BF).astype(F32)
    row = iota((EXTRA, SLOTS), 0)
    parts = jnp.where(row == 0, hi, jnp.where(row == 1, mid, squares - hi - mid))
    parts = jnp.where(row < 3, parts, 0.0).astype(BF)
    out_ref[SLOTS:, :] = jnp.concatenate([parts, parts], axis=1)


def own_body(w_ref, w2_ref, x_ref, out_ref, squares_ref):
    products(x_ref, (w_ref, w2_ref), out_ref)
    squares_ref[...] = jnp.broadcast_to(sums_of_squares(x_ref), (8, SLOTS))


def act_body(own_ref, squares_ref, got_ref, out_ref):
    diagonal = iota((128, 128), 0) == iota((128, 128), 1)
    got = jnp.sum(got_ref[SLOTS:, :SLOTS].astype(F32), axis=0, keepdims=True)
    squares = squares_ref[0:1, :] + got
    for t in range(SLOTS // 128):
        rows = slice(t * 128, (t + 1) * 128)
        column = jnp.sum(jnp.where(diagonal, squares[:, rows], 0.0), axis=1, keepdims=True)
        inv_rms = lax.rsqrt(column / D + 1e-05)
        hidden = (own_ref[rows, :] + got_ref[rows, :].astype(F32)) * inv_rms
        for k in range(NC):
            gate = hidden[:, 256 * k : 256 * k + 128]
            up = hidden[:, 256 * k + 128 : 256 * k + 256]
            act = (gate / (1.0 + jnp.exp(-gate)) * up).astype(BF)
            for z in range(NZ):
                out_ref[z, rows, 128 * k : 128 * (k + 1)] = act


def down_body(place_ref, own_ref, other_ref, x_ref, out_ref):
    rows = FEATS // PACK
    group = iota((rows, 128), 1) // PIECE
    core = place_ref[NYL]
    for k, w_ref in enumerate((own_ref, other_ref)):
        out = jnp.zeros((w_ref.shape[0], SLOTS), F32)
        for z in range(NZ):
            units = x_ref[z]
            if k == 1:
                units = jnp.concatenate([units[:, 128:], units[:, :128]], axis=1)
            out += dot(w_ref[:, z * 256 : (z + 1) * 256], units, NT)
        to = core if k == 0 else 1 - core
        for j in range(NYL):
            for t in range(EXPERTS // PACK):
                tile = out[j * FEATS : (j + 1) * FEATS, t * 128 : (t + 1) * 128]
                for i in range(PACK):
                    packed = jnp.zeros((rows, 128), F32)
                    for q in range(PACK):
                        part = tile[q * rows : (q + 1) * rows, :]
                        shift = (q - i) % PACK * PIECE
                        part = pltpu.roll(part, shift, 1) if shift else part
                        packed = jnp.where(group == q, part, packed)
                    out_ref[t * PACK + i, j, to] = packed.astype(BF)


def combine_body(target_ref, gates_ref, in_ref, out_ref):
    rows = FEATS // PACK
    target = jnp.concatenate([target_ref[0:1, :], target_ref[1:2, :]], axis=1)
    slot = iota((128, 2 * ROW_DEV), 0) % PIECE
    group = iota((rows, 128), 1) // PIECE
    picked = jnp.zeros((FEATS, 2 * ROW_DEV), F32)
    for e in range(EXPERTS):
        for h in range(NC):
            place = one_hot(target - (e * CAP + h * PIECE) == slot)
            total = in_ref[e, 0, h].astype(F32)
            for j in range(1, NYL):
                total += in_ref[e, j, h].astype(F32)
            total = jnp.concatenate([jnp.where(group == q, total, 0.0) for q in range(PACK)], axis=0)
            hi = total.astype(BF)
            rest = (total - hi.astype(F32)).astype(BF)
            picked += dot(hi, place) + dot(rest, place)
    mixed = gates_ref[0:1, :] * picked[:, :ROW_DEV] + gates_ref[1:2, :] * picked[:, ROW_DEV:]
    out_ref[...] = mixed.astype(BF)


def cut_body(place_ref, in_ref, *out_refs):
    width = out_refs[0].shape[1]
    for m, out_ref in enumerate(out_refs):
        start = pl.multiple_of(place_ref[m] * width, width)
        out_ref[...] = in_ref[:, pl.ds(start, width)]


def join_body(place_ref, *refs):
    pieces, out_ref = refs[:NYL], refs[NYL]
    core = place_ref[NYL]
    for m, piece in enumerate(pieces):
        rows = pl.ds(pl.multiple_of(place_ref[m] * FEATS, FEATS), FEATS)
        for z in range(NZ):
            for k, at in enumerate((core, 1 - core)):
                cols = pl.ds(pl.multiple_of((2 * z + at) * 128, 128), 128)
                start = (2 * z + k) * 128
                out_ref[rows, start : start + 128] = piece[:, cols]


def per_device(hidden_state, norm_gain, routes, gates, w_gate, w_up, w_down):
    quarter = 2 * lax.axis_index("ya") + lax.axis_index("yb")
    core = lax.axis_index("c")
    swap = [(0, 1), (1, 0)]
    places = [quarter ^ m for m in range(NYL)] + [core, lax.axis_index("yb")]
    places = jnp.stack(places).astype(I32)

    outgoing, targets = call(
        dispatch_body,
        (
            jax.ShapeDtypeStruct((EXPERTS, NYA, NC, PIECE, ROW_DEV), BF),
            jax.ShapeDtypeStruct((8, ROW_DEV), I32),
        ),
        hidden_state.T,
        norm_gain[None, :],
        routes.T,
    )
    with jax.named_scope("rows_over_xyc"):
        incoming = lax.all_to_all(
            outgoing.reshape(EXPERTS * GROUP, PIECE, ROW_DEV),
            ("x", "yh", "ya", "c"),
            split_axis=0,
            concat_axis=0,
            tiled=True,
        )
    incoming = incoming.reshape(EXPERTS, GROUP, PIECE, ROW_DEV)
    block = call(
        turn_body,
        jax.ShapeDtypeStruct((NZ, DEPTH, 128), BF),
        incoming,
        scratch_shapes=[pltpu.VMEM((DEPTH, 128), BF)],
    )
    with jax.named_scope("features_over_z"):
        features = lax.all_to_all(block, "z", split_axis=0, concat_axis=0, tiled=True)

    split = (NYA, NYB, NZ, NC * FEATS, 128)
    half = jax.ShapeDtypeStruct((2, NYA, NZ, NC * FEATS, 128), BF)
    gate_cols, up_cols = w_gate[0].reshape(split), w_up[0].reshape(split)
    w_own, w_sent = call(halves_body, (half, half), places, gate_cols, up_cols, scalars=1)
    w_sent, _ = lax.optimization_barrier((w_sent, block))
    with jax.named_scope("gate_up_over_y"):
        w_next = lax.ppermute(w_sent, "yb", swap)
    down = w_down[0]
    units = down.shape[0] // NYL
    piece = jax.ShapeDtypeStruct((FEATS, units), BF)
    pieces = list(call(cut_body, (piece,) * NYL, places, down.T, scalars=1))

    def over_y(m, after):
        sent, _ = lax.optimization_barrier((pieces[m], after))
        with jax.named_scope("down_over_y"):
            return lax.ppermute(sent, ("ya", "yb"), [(i, i ^ m) for i in range(NYL)])

    pieces[2] = over_y(2, block)
    w_next, pieces[2] = lax.optimization_barrier((w_next, pieces[2]))
    pieces[1] = over_y(1, w_next)
    with jax.named_scope("gate_up_over_c"):
        w_core = lax.ppermute(w_own, "c", swap)
        w_next_core = lax.ppermute(w_next, "c", swap)

    flops = 2 * SLOTS * D // 2 * 512
    sent = call(
        neighbour_body,
        jax.ShapeDtypeStruct((SLOTS + EXTRA, 512), BF),
        w_next,
        w_next_core,
        features,
        flops=flops,
        moved=5_000_000,
        scratch_shapes=[pltpu.VMEM((SLOTS, 512), F32)],
    )
    with jax.named_scope("hidden_over_y"):
        got = lax.ppermute(sent, "yb", swap)
    own, squares = call(
        own_body,
        (jax.ShapeDtypeStruct((SLOTS, 512), F32), jax.ShapeDtypeStruct((8, SLOTS), F32)),
        w_own,
        w_core,
        features,
        flops=flops,
        moved=5_000_000,
    )
    acts = call(act_body, jax.ShapeDtypeStruct((NZ, SLOTS, 256), BF), own, squares, got)
    with jax.named_scope("units_over_z"):
        acts = lax.all_to_all(acts, "z", split_axis=0, concat_axis=0, tiled=True)

    pieces[3] = over_y(3, own)
    part = jax.ShapeDtypeStruct((NYL * FEATS, units), BF)
    down_own = call(join_body, part, places, *pieces, scalars=1)
    with jax.named_scope("down_over_c"):
        down_other = lax.ppermute(down_own, "c", swap)

    rows = FEATS // PACK
    out = call(
        down_body,
        jax.ShapeDtypeStruct((EXPERTS, NYL, NC, rows, 128), BF),
        places,
        down_own,
        down_other,
        acts,
        scalars=1,
        flops=2 * NC * NYL * FEATS * units * SLOTS,
        moved=5_000_000,
    )
    with jax.named_scope("out_over_xyc"):
        back = lax.all_to_all(
            out.reshape(EXPERTS * NYL * NC, rows, 128),
            ("x", "yh", "ya", "yb", "c"),
            split_axis=0,
            concat_axis=0,
            tiled=True,
        )
    back = back.reshape(EXPERTS, NYL, NC, rows, 128)
    return call(
        combine_body, jax.ShapeDtypeStruct((FEATS, ROW_DEV), BF), targets, gates.T, back
    ).T


def solution(mesh):
    fine = Mesh(
        mesh.devices.reshape(NX, NYH, NYA, NYB, NZ, NC), ("x", "yh", "ya", "yb", "z", "c")
    )
    exp, tp = ("x", "yh"), ("ya", "yb", "z", "c")
    in_specs = (
        P(exp, tp),
        P(tp),
        P(exp, None),
        P(exp, None),
        P(exp, None, tp),
        P(exp, None, tp),
        P(exp, None, tp),
    )
    return jax.shard_map(
        per_device, mesh=fine, in_specs=in_specs, out_specs=P(exp, tp), check_vma=False
    )
```

```python
import functools

import jax
import jax.numpy as jnp
from jax import lax
from jax.experimental import pallas as pl
from jax.experimental.pallas import tpu as pltpu
from jax.sharding import Mesh, PartitionSpec as P

D = 6144
EXPERTS = 8
NX, NYH, NYA, NYB, NZ, NC = 4, 2, 2, 2, 8, 2
NYL = NYA * NYB
NZC = NZ * NC
FEATS = 96
GROUP = NYA * NC
ROW_DEV = 128
CAP = 64
PIECE = CAP // NC
SLOTS = EXPERTS * PIECE
EXTRA = 16
TILES = GROUP * FEATS // 128
PARTS = SLOTS // 128 * 8
DEPTH = TILES * SLOTS + PARTS
PACK = 128 // PIECE
BF = jnp.bfloat16
F32 = jnp.float32
I32 = jnp.int32
BIG = 3.0e38
NT = (((1,), (1,)), ((), ()))
VMEM_LIMIT = 40 * 1024 * 1024


def iota(shape, dim):
    return lax.broadcasted_iota(I32, shape, dim)


def one_hot(condition):
    return jnp.where(condition, 1.0, 0.0).astype(BF)


def dot(a, b, dims=(((1,), (0,)), ((), ()))):
    return lax.dot_general(a, b, dims, preferred_element_type=F32)


def call(body, out_shape, *args, flops=1_000_000, moved=1_000_000, scalars=0, after=(), **kw):
    specs = [pl.BlockSpec(memory_space=pltpu.SMEM)] * scalars
    specs += [pl.BlockSpec(memory_space=pltpu.VMEM)] * (len(args) - scalars)
    specs += [pl.BlockSpec(memory_space=pl.ANY)] * len(after)
    return pl.pallas_call(
        body,
        out_shape=out_shape,
        in_specs=specs,
        out_specs=jax.tree.map(lambda _: pl.BlockSpec(memory_space=pltpu.VMEM), out_shape),
        compiler_params=pltpu.CompilerParams(vmem_limit_bytes=VMEM_LIMIT),
        cost_estimate=pl.CostEstimate(flops=flops, bytes_accessed=moved, transcendentals=0),
        **kw,
    )(*args, *after)


def dispatch_body(hidden_hbm, gain_hbm, routes_hbm, out_ref, target_ref, hidden_ref, gain_ref, routes_ref, sem):
    pairs = ((routes_hbm, routes_ref), (hidden_hbm, hidden_ref), (gain_hbm, gain_ref))
    copies = [pltpu.make_async_copy(a, b, sem.at[i]) for i, (a, b) in enumerate(pairs)]
    for copy in copies:
        copy.start()
    for copy in copies:
        copy.wait()
    diagonal = iota((FEATS, FEATS), 0) == iota((FEATS, FEATS), 1)
    gain = jnp.sum(jnp.where(diagonal, gain_ref[...].astype(F32), 0.0), axis=1, keepdims=True)
    values = hidden_ref[...].astype(F32)
    scaled = jnp.clip(values * gain, -BIG, BIG)
    squares = jnp.minimum(jnp.sum(values * values, axis=0, keepdims=True), BIG)
    hi = squares.astype(BF).astype(F32)
    mid = (squares - hi).astype(BF).astype(F32)
    low = squares - hi - mid
    row = iota((ROW_DEV - FEATS, ROW_DEV), 0)
    parts = jnp.where(row == 0, hi, jnp.where(row == 1, mid, jnp.where(row == 2, low, 0.0)))
    rows = jnp.concatenate([scaled, parts], axis=0).astype(BF)

    first, second = routes_ref[0:1, :], routes_ref[1:2, :]
    expert = iota((2 * EXPERTS, ROW_DEV), 0)
    named0, named1 = expert == first, expert == second
    earlier = one_hot(iota((ROW_DEV, ROW_DEV), 0) < iota((ROW_DEV, ROW_DEV), 1))
    before = dot(one_hot(named0 | named1), earlier)
    rank0 = jnp.sum(jnp.where(named0, before, 0.0), axis=0, keepdims=True).astype(I32)
    rank1 = jnp.sum(jnp.where(named1, before, 0.0), axis=0, keepdims=True).astype(I32)
    target0, target1 = first * CAP + rank0, second * CAP + rank1
    target_ref[...] = jnp.where(iota((8, ROW_DEV), 0) == 0, target0, target1)
    slot = iota((EXPERTS * CAP, ROW_DEV), 0)
    place = one_hot((slot == target0) | (slot == target1))
    sent = dot(place, rows, NT).astype(BF).reshape(EXPERTS, NC, PIECE, ROW_DEV)
    for j in range(NYA):
        out_ref[:, j] = sent


def turn_body(in_ref, out_ref, turned_ref):
    row, lane = iota((EXTRA, ROW_DEV), 0), iota((EXTRA, ROW_DEV), 1)
    source, column = iota((ROW_DEV, ROW_DEV), 0), iota((ROW_DEV, ROW_DEV), 1)
    extra = jnp.zeros((EXTRA, SLOTS), F32)
    rows = [in_ref[:, j].reshape(SLOTS, ROW_DEV) for j in range(GROUP)]
    for t in range(TILES):
        tile = jnp.zeros((SLOTS, ROW_DEV), F32)
        for j in range(GROUP):
            shift = t * ROW_DEV - j * FEATS
            if -ROW_DEV < shift < FEATS:
                pick = one_hot((source - column == shift) & (source < FEATS))
                tile += dot(rows[j], pick)
        turned_ref[t * SLOTS : (t + 1) * SLOTS, :] = tile.astype(BF)
    for j in range(GROUP):
        pick = one_hot((row == lane - FEATS) & (row < 3))
        extra += dot(pick, rows[j], NT)
    squares = jnp.minimum(jnp.sum(extra, axis=0, keepdims=True), BIG)
    hi = squares.astype(BF).astype(F32)
    mid = (squares - hi).astype(BF).astype(F32)
    row = iota((8, SLOTS), 0)
    extra = jnp.where(row == 0, hi, jnp.where(row == 1, mid, squares - hi - mid))
    extra = jnp.where(row < 3, extra, 0.0)
    tiles = [extra[:, t * 128 : (t + 1) * 128] for t in range(SLOTS // 128)]
    turned_ref[TILES * SLOTS :, :] = jnp.concatenate(tiles, axis=0).astype(BF)
    for z in range(NZ):
        out_ref[z] = turned_ref[...]


def halves_body(place_ref, gate_ref, up_ref, own_ref, other_ref):
    parity = place_ref[NYL + 1]
    for i, ref in enumerate((gate_ref, up_ref)):
        for j in range(NYA):
            own_ref[i, j] = ref[j, parity]
            other_ref[i, j] = ref[j, 1 - parity]


def products(x_ref, weight_refs, acc_ref):
    for z in range(0, NZ, 2):
        tiles, columns = [], []
        for i in range(z, z + 2):
            tiles += [x_ref[i, t * SLOTS : (t + 1) * SLOTS, :] for t in range(TILES)]
            weights = [w[k, :, i].reshape(GROUP * FEATS, 128) for w in weight_refs for k in range(2)]
            columns.append(jnp.concatenate(weights, axis=1))
        total = dot(jnp.concatenate(tiles, axis=1), jnp.concatenate(columns, axis=0))
        if z == 0:
            acc_ref[...] = total
        else:
            acc_ref[...] += total


def sums_of_squares(x_ref):
    parts = jnp.zeros((PARTS, 128), F32)
    for z in range(NZ):
        parts += x_ref[z, TILES * SLOTS :, :].astype(F32)
    sums = [
        jnp.sum(parts[t * 8 : (t + 1) * 8], axis=0, keepdims=True) for t in range(SLOTS // 128)
    ]
    return jnp.concatenate(sums, axis=1)


def neighbour_body(w_ref, w2_ref, x_ref, *rest):
    out_ref, acc_ref = rest[-2:]
    products(x_ref, (w_ref, w2_ref), acc_ref)
    out_ref[:SLOTS, :] = acc_ref[...].astype(BF)
    squares = jnp.minimum(sums_of_squares(x_ref), BIG)
    hi = squares.astype(BF).astype(F32)
    mid = (squares - hi).astype(BF).astype(F32)
    row = iota((EXTRA, SLOTS), 0)
    parts = jnp.where(row == 0, hi, jnp.where(row == 1, mid, squares - hi - mid))
    parts = jnp.where(row < 3, parts, 0.0).astype(BF)
    out_ref[SLOTS:, :] = jnp.concatenate([parts, parts], axis=1)


def own_body(w_ref, w2_ref, x_ref, out_ref, squares_ref):
    products(x_ref, (w_ref, w2_ref), out_ref)
    squares_ref[...] = jnp.broadcast_to(sums_of_squares(x_ref), (8, SLOTS))


def act_body(own_ref, squares_ref, got_ref, out_ref):
    diagonal = iota((128, 128), 0) == iota((128, 128), 1)
    got = jnp.sum(got_ref[SLOTS:, :SLOTS].astype(F32), axis=0, keepdims=True)
    squares = squares_ref[0:1, :] + got
    for t in range(SLOTS // 128):
        rows = slice(t * 128, (t + 1) * 128)
        column = jnp.sum(jnp.where(diagonal, squares[:, rows], 0.0), axis=1, keepdims=True)
        inv_rms = lax.rsqrt(column / D + 1e-05)
        hidden = (own_ref[rows, :] + got_ref[rows, :].astype(F32)) * inv_rms
        for k in range(NC):
            gate = hidden[:, 256 * k : 256 * k + 128]
            up = hidden[:, 256 * k + 128 : 256 * k + 256]
            act = (gate / (1.0 + jnp.exp(-gate)) * up).astype(BF)
            for z in range(NZ):
                out_ref[z, rows, 128 * k : 128 * (k + 1)] = act


def down_body(place_ref, own_ref, other_ref, x_ref, out_ref):
    rows = FEATS // PACK
    group = iota((rows, 128), 1) // PIECE
    core = place_ref[NYL]
    for k, w_ref in enumerate((own_ref, other_ref)):
        out = jnp.zeros((w_ref.shape[0], SLOTS), F32)
        for z in range(NZ):
            units = x_ref[z]
            if k == 1:
                units = jnp.concatenate([units[:, 128:], units[:, :128]], axis=1)
            out += dot(w_ref[:, z * 256 : (z + 1) * 256], units, NT)
        to = core if k == 0 else 1 - core
        for j in range(NYL):
            for t in range(EXPERTS // PACK):
                tile = out[j * FEATS : (j + 1) * FEATS, t * 128 : (t + 1) * 128]
                for i in range(PACK):
                    packed = jnp.zeros((rows, 128), F32)
                    for q in range(PACK):
                        part = tile[q * rows : (q + 1) * rows, :]
                        shift = (q - i) % PACK * PIECE
                        part = pltpu.roll(part, shift, 1) if shift else part
                        packed = jnp.where(group == q, part, packed)
                    out_ref[t * PACK + i, j, to] = packed.astype(BF)


def combine_body(target_ref, gates_ref, in_ref, out_ref):
    rows = FEATS // PACK
    target = jnp.concatenate([target_ref[0:1, :], target_ref[1:2, :]], axis=1)
    slot = iota((128, 2 * ROW_DEV), 0) % PIECE
    group = iota((rows, 128), 1) // PIECE
    picked = jnp.zeros((FEATS, 2 * ROW_DEV), F32)
    for e in range(EXPERTS):
        for h in range(NC):
            place = one_hot(target - (e * CAP + h * PIECE) == slot)
            total = in_ref[e, 0, h].astype(F32)
            for j in range(1, NYL):
                total += in_ref[e, j, h].astype(F32)
            total = jnp.concatenate([jnp.where(group == q, total, 0.0) for q in range(PACK)], axis=0)
            hi = total.astype(BF)
            rest = (total - hi.astype(F32)).astype(BF)
            picked += dot(hi, place) + dot(rest, place)
    mixed = gates_ref[0:1, :] * picked[:, :ROW_DEV] + gates_ref[1:2, :] * picked[:, ROW_DEV:]
    out_ref[...] = mixed.astype(BF)


def cut_body(place_ref, in_ref, *out_refs):
    width = out_refs[0].shape[1]
    for m, out_ref in enumerate(out_refs):
        start = pl.multiple_of(place_ref[m] * width, width)
        out_ref[...] = in_ref[:, pl.ds(start, width)]


def join_body(place_ref, *refs):
    pieces, out_ref = refs[:NYL], refs[NYL]
    core = place_ref[NYL]
    for m, piece in enumerate(pieces):
        rows = pl.ds(pl.multiple_of(place_ref[m] * FEATS, FEATS), FEATS)
        for z in range(NZ):
            for k, at in enumerate((core, 1 - core)):
                cols = pl.ds(pl.multiple_of((2 * z + at) * 128, 128), 128)
                start = (2 * z + k) * 128
                out_ref[rows, start : start + 128] = piece[:, cols]


def per_device(hidden_state, norm_gain, routes, gates, w_gate, w_up, w_down):
    quarter = 2 * lax.axis_index("ya") + lax.axis_index("yb")
    core = lax.axis_index("c")
    swap = [(0, 1), (1, 0)]
    places = [quarter ^ m for m in range(NYL)] + [core, lax.axis_index("yb")]
    places = jnp.stack(places).astype(I32)

    hbm, vmem = (pl.BlockSpec(memory_space=space) for space in (pltpu.HBM, pltpu.VMEM))
    outgoing, targets = pl.pallas_call(
        dispatch_body,
        out_shape=(
            jax.ShapeDtypeStruct((EXPERTS, NYA, NC, PIECE, ROW_DEV), BF),
            jax.ShapeDtypeStruct((8, ROW_DEV), I32),
        ),
        in_specs=[hbm, hbm, hbm],
        out_specs=(vmem, vmem),
        scratch_shapes=[
            pltpu.VMEM((FEATS, ROW_DEV), BF),
            pltpu.VMEM((1, FEATS), BF),
            pltpu.VMEM((2, ROW_DEV), I32),
            pltpu.SemaphoreType.DMA((3,)),
        ],
        compiler_params=pltpu.CompilerParams(vmem_limit_bytes=62 * 1024 * 1024),
        cost_estimate=pl.CostEstimate(flops=1_000_000, bytes_accessed=1_000_000, transcendentals=0),
    )(hidden_state.T, norm_gain[None, :], routes.T)
    with jax.named_scope("rows_over_xyc"):
        incoming = lax.all_to_all(
            outgoing.reshape(EXPERTS * GROUP, PIECE, ROW_DEV),
            ("x", "yh", "ya", "c"),
            split_axis=0,
            concat_axis=0,
            tiled=True,
        )
    incoming = incoming.reshape(EXPERTS, GROUP, PIECE, ROW_DEV)
    block = call(
        turn_body,
        jax.ShapeDtypeStruct((NZ, DEPTH, 128), BF),
        incoming,
        scratch_shapes=[pltpu.VMEM((DEPTH, 128), BF)],
    )
    with jax.named_scope("features_over_z"):
        features = lax.all_to_all(block, "z", split_axis=0, concat_axis=0, tiled=True)

    split = (NYA, NYB, NZ, NC * FEATS, 128)
    half = jax.ShapeDtypeStruct((2, NYA, NZ, NC * FEATS, 128), BF)
    gate_cols, up_cols = w_gate[0].reshape(split), w_up[0].reshape(split)
    w_own, w_sent = call(halves_body, (half, half), places, gate_cols, up_cols, scalars=1)
    with jax.named_scope("gate_up_over_y"):
        w_next = lax.ppermute(w_sent, "yb", swap)
    down = w_down[0]
    units = down.shape[0] // NYL
    piece = jax.ShapeDtypeStruct((FEATS, units), BF)
    pieces = list(call(cut_body, (piece,) * NYL, places, down.T, scalars=1))

    def over_y(m, after):
        sent, _ = lax.optimization_barrier((pieces[m], after))
        with jax.named_scope("down_over_y"):
            return lax.ppermute(sent, ("ya", "yb"), [(i, i ^ m) for i in range(NYL)])

    pieces[2] = over_y(2, block)
    w_own, _ = lax.optimization_barrier((w_own, block))
    with jax.named_scope("gate_up_over_c"):
        w_core = lax.ppermute(w_own, "c", swap)
    w_next, pieces[2], w_core = lax.optimization_barrier((w_next, pieces[2], w_core))
    pieces[1] = over_y(1, w_next)
    with jax.named_scope("gate_up_over_c"):
        w_next_core = lax.ppermute(w_next, "c", swap)

    flops = 2 * SLOTS * D // 2 * 512
    own, squares = call(
        own_body,
        (jax.ShapeDtypeStruct((SLOTS, 512), F32), jax.ShapeDtypeStruct((8, SLOTS), F32)),
        w_own,
        w_core,
        features,
        flops=flops,
        moved=5_000_000,
    )
    sent = call(
        neighbour_body,
        jax.ShapeDtypeStruct((SLOTS + EXTRA, 512), BF),
        w_next,
        w_next_core,
        features,
        flops=flops,
        moved=5_000_000,
        after=(squares,),
        scratch_shapes=[pltpu.VMEM((SLOTS, 512), F32)],
    )
    with jax.named_scope("hidden_over_y"):
        got = lax.ppermute(sent, "yb", swap)
    acts = call(act_body, jax.ShapeDtypeStruct((NZ, SLOTS, 256), BF), own, squares, got)
    with jax.named_scope("units_over_z"):
        acts = lax.all_to_all(acts, "z", split_axis=0, concat_axis=0, tiled=True)

    pieces[3] = over_y(3, own)
    part = jax.ShapeDtypeStruct((NYL * FEATS, units), BF)
    down_own = call(join_body, part, places, *pieces, scalars=1)
    with jax.named_scope("down_over_c"):
        down_other = lax.ppermute(down_own, "c", swap)

    rows = FEATS // PACK
    out = call(
        down_body,
        jax.ShapeDtypeStruct((EXPERTS, NYL, NC, rows, 128), BF),
        places,
        down_own,
        down_other,
        acts,
        scalars=1,
        flops=2 * NC * NYL * FEATS * units * SLOTS,
        moved=5_000_000,
    )
    with jax.named_scope("out_over_xyc"):
        back = lax.all_to_all(
            out.reshape(EXPERTS * NYL * NC, rows, 128),
            ("x", "yh", "ya", "yb", "c"),
            split_axis=0,
            concat_axis=0,
            tiled=True,
        )
    back = back.reshape(EXPERTS, NYL, NC, rows, 128)
    return call(
        combine_body, jax.ShapeDtypeStruct((FEATS, ROW_DEV), BF), targets, gates.T, back
    ).T


def solution(mesh):
    fine = Mesh(
        mesh.devices.reshape(NX, NYH, NYA, NYB, NZ, NC), ("x", "yh", "ya", "yb", "z", "c")
    )
    exp, tp = ("x", "yh"), ("ya", "yb", "z", "c")
    in_specs = (
        P(exp, tp),
        P(tp),
        P(exp, None),
        P(exp, None),
        P(exp, None, tp),
        P(exp, None, tp),
        P(exp, None, tp),
    )
    return jax.shard_map(
        per_device, mesh=fine, in_specs=in_specs, out_specs=P(exp, tp), check_vma=False
    )
```

```python
import functools

import jax
import jax.numpy as jnp
from jax import lax
from jax.experimental import pallas as pl
from jax.experimental.pallas import tpu as pltpu
from jax.sharding import Mesh, PartitionSpec as P

D = 6144
EXPERTS = 8
NX, NYH, NYA, NYB, NZ, NC = 4, 2, 2, 2, 8, 2
NYL = NYA * NYB
NZC = NZ * NC
FEATS = 96
GROUP = NYA * NC
ROW_DEV = 128
CAP = 64
PIECE = CAP // NC
SLOTS = EXPERTS * PIECE
EXTRA = 16
TILES = GROUP * FEATS // 128
PARTS = SLOTS // 128 * 8
DEPTH = TILES * SLOTS + PARTS
PACK = 128 // PIECE
BF = jnp.bfloat16
F32 = jnp.float32
I32 = jnp.int32
BIG = 3.0e38
NT = (((1,), (1,)), ((), ()))
WHOLE_VMEM = 62 * 1024 * 1024
VMEM_LIMIT = 40 * 1024 * 1024


def iota(shape, dim):
    return lax.broadcasted_iota(I32, shape, dim)


def one_hot(condition):
    return jnp.where(condition, 1.0, 0.0).astype(BF)


def dot(a, b, dims=(((1,), (0,)), ((), ()))):
    return lax.dot_general(a, b, dims, preferred_element_type=F32)


def call(body, out_shape, *args, flops=1_000_000, moved=1_000_000, scalars=0, after=(), limit=VMEM_LIMIT, **kw):
    specs = [pl.BlockSpec(memory_space=pltpu.SMEM)] * scalars
    specs += [pl.BlockSpec(memory_space=pltpu.VMEM)] * (len(args) - scalars)
    specs += [pl.BlockSpec(memory_space=pl.ANY)] * len(after)
    return pl.pallas_call(
        body,
        out_shape=out_shape,
        in_specs=specs,
        out_specs=jax.tree.map(lambda _: pl.BlockSpec(memory_space=pltpu.VMEM), out_shape),
        compiler_params=pltpu.CompilerParams(vmem_limit_bytes=limit),
        cost_estimate=pl.CostEstimate(flops=flops, bytes_accessed=moved, transcendentals=0),
        **kw,
    )(*args, *after)


def dispatch_body(hidden_ref, gain_ref, routes_ref, out_ref, target_ref):
    diagonal = iota((FEATS, FEATS), 0) == iota((FEATS, FEATS), 1)
    gain = jnp.sum(jnp.where(diagonal, gain_ref[...].astype(F32), 0.0), axis=1, keepdims=True)
    values = hidden_ref[...].astype(F32)
    scaled = jnp.clip(values * gain, -BIG, BIG)
    squares = jnp.minimum(jnp.sum(values * values, axis=0, keepdims=True), BIG)
    hi = squares.astype(BF).astype(F32)
    mid = (squares - hi).astype(BF).astype(F32)
    low = squares - hi - mid
    row = iota((ROW_DEV - FEATS, ROW_DEV), 0)
    parts = jnp.where(row == 0, hi, jnp.where(row == 1, mid, jnp.where(row == 2, low, 0.0)))
    rows = jnp.concatenate([scaled, parts], axis=0).astype(BF)

    first, second = routes_ref[0:1, :], routes_ref[1:2, :]
    expert = iota((2 * EXPERTS, ROW_DEV), 0)
    named0, named1 = expert == first, expert == second
    earlier = one_hot(iota((ROW_DEV, ROW_DEV), 0) < iota((ROW_DEV, ROW_DEV), 1))
    before = dot(one_hot(named0 | named1), earlier)
    rank0 = jnp.sum(jnp.where(named0, before, 0.0), axis=0, keepdims=True).astype(I32)
    rank1 = jnp.sum(jnp.where(named1, before, 0.0), axis=0, keepdims=True).astype(I32)
    target0, target1 = first * CAP + rank0, second * CAP + rank1
    target_ref[...] = jnp.where(iota((8, ROW_DEV), 0) == 0, target0, target1)
    slot = iota((EXPERTS * CAP, ROW_DEV), 0)
    place = one_hot((slot == target0) | (slot == target1))
    sent = dot(place, rows, NT).astype(BF).reshape(EXPERTS, NC, PIECE, ROW_DEV)
    for j in range(NYA):
        out_ref[:, j] = sent


def turn_body(in_ref, out_ref, turned_ref):
    row, lane = iota((EXTRA, ROW_DEV), 0), iota((EXTRA, ROW_DEV), 1)
    source, column = iota((ROW_DEV, ROW_DEV), 0), iota((ROW_DEV, ROW_DEV), 1)
    extra = jnp.zeros((EXTRA, SLOTS), F32)
    rows = [in_ref[:, j].reshape(SLOTS, ROW_DEV) for j in range(GROUP)]
    for t in range(TILES):
        tile = jnp.zeros((SLOTS, ROW_DEV), F32)
        for j in range(GROUP):
            shift = t * ROW_DEV - j * FEATS
            if -ROW_DEV < shift < FEATS:
                pick = one_hot((source - column == shift) & (source < FEATS))
                tile += dot(rows[j], pick)
        turned_ref[t * SLOTS : (t + 1) * SLOTS, :] = tile.astype(BF)
    for j in range(GROUP):
        pick = one_hot((row == lane - FEATS) & (row < 3))
        extra += dot(pick, rows[j], NT)
    squares = jnp.minimum(jnp.sum(extra, axis=0, keepdims=True), BIG)
    hi = squares.astype(BF).astype(F32)
    mid = (squares - hi).astype(BF).astype(F32)
    row = iota((8, SLOTS), 0)
    extra = jnp.where(row == 0, hi, jnp.where(row == 1, mid, squares - hi - mid))
    extra = jnp.where(row < 3, extra, 0.0)
    tiles = [extra[:, t * 128 : (t + 1) * 128] for t in range(SLOTS // 128)]
    turned_ref[TILES * SLOTS :, :] = jnp.concatenate(tiles, axis=0).astype(BF)
    for z in range(NZ):
        out_ref[z] = turned_ref[...]


def half_body(own, place_ref, gate_ref, up_ref, out_ref, held_ref, sem):
    parity = place_ref[NYL + 1] if own else 1 - place_ref[NYL + 1]
    parts = [(i, j, ref) for i, ref in enumerate((gate_ref, up_ref)) for j in range(NYA)]
    to_held, to_out = [], []
    for k, (i, j, ref) in enumerate(parts):
        to_held.append(pltpu.make_async_copy(ref.at[j, parity], held_ref.at[i, j], sem.at[k]))
        to_out.append(pltpu.make_async_copy(held_ref.at[i, j], out_ref.at[i, j], sem.at[len(parts) + k]))
        to_held[-1].start()
    for first, second in zip(to_held, to_out):
        first.wait()
        second.start()
    for second in to_out:
        second.wait()


def products(x_ref, weight_refs, acc_ref):
    for z in range(0, NZ, 2):
        tiles, columns = [], []
        for i in range(z, z + 2):
            tiles += [x_ref[i, t * SLOTS : (t + 1) * SLOTS, :] for t in range(TILES)]
            weights = [w[k, :, i].reshape(GROUP * FEATS, 128) for w in weight_refs for k in range(2)]
            columns.append(jnp.concatenate(weights, axis=1))
        total = dot(jnp.concatenate(tiles, axis=1), jnp.concatenate(columns, axis=0))
        if z == 0:
            acc_ref[...] = total
        else:
            acc_ref[...] += total


def sums_of_squares(x_ref):
    parts = jnp.zeros((PARTS, 128), F32)
    for z in range(NZ):
        parts += x_ref[z, TILES * SLOTS :, :].astype(F32)
    sums = [
        jnp.sum(parts[t * 8 : (t + 1) * 8], axis=0, keepdims=True) for t in range(SLOTS // 128)
    ]
    return jnp.concatenate(sums, axis=1)


def neighbour_body(w_ref, w2_ref, x_ref, out_ref, acc_ref):
    products(x_ref, (w_ref, w2_ref), acc_ref)
    out_ref[:SLOTS, :] = acc_ref[...].astype(BF)
    squares = jnp.minimum(sums_of_squares(x_ref), BIG)
    hi = squares.astype(BF).astype(F32)
    mid = (squares - hi).astype(BF).astype(F32)
    row = iota((EXTRA, SLOTS), 0)
    parts = jnp.where(row == 0, hi, jnp.where(row == 1, mid, squares - hi - mid))
    parts = jnp.where(row < 3, parts, 0.0).astype(BF)
    out_ref[SLOTS:, :] = jnp.concatenate([parts, parts], axis=1)


def own_body(w_ref, w2_ref, x_ref, out_ref, squares_ref):
    products(x_ref, (w_ref, w2_ref), out_ref)
    squares_ref[...] = jnp.broadcast_to(sums_of_squares(x_ref), (8, SLOTS))


def act_body(own_ref, squares_ref, got_ref, out_ref):
    diagonal = iota((128, 128), 0) == iota((128, 128), 1)
    got = jnp.sum(got_ref[SLOTS:, :SLOTS].astype(F32), axis=0, keepdims=True)
    squares = squares_ref[0:1, :] + got
    for t in range(SLOTS // 128):
        rows = slice(t * 128, (t + 1) * 128)
        column = jnp.sum(jnp.where(diagonal, squares[:, rows], 0.0), axis=1, keepdims=True)
        inv_rms = lax.rsqrt(column / D + 1e-05)
        hidden = (own_ref[rows, :] + got_ref[rows, :].astype(F32)) * inv_rms
        for k in range(NC):
            gate = hidden[:, 256 * k : 256 * k + 128]
            up = hidden[:, 256 * k + 128 : 256 * k + 256]
            act = (gate / (1.0 + jnp.exp(-gate)) * up).astype(BF)
            for z in range(NZ):
                out_ref[z, rows, 128 * k : 128 * (k + 1)] = act


def down_body(place_ref, own_ref, other_ref, x_ref, out_ref):
    rows = FEATS // PACK
    group = iota((rows, 128), 1) // PIECE
    core = place_ref[NYL]
    for k, w_ref in enumerate((own_ref, other_ref)):
        out = jnp.zeros((w_ref.shape[0], SLOTS), F32)
        for z in range(NZ):
            units = x_ref[z]
            if k == 1:
                units = jnp.concatenate([units[:, 128:], units[:, :128]], axis=1)
            out += dot(w_ref[:, z * 256 : (z + 1) * 256], units, NT)
        to = core if k == 0 else 1 - core
        for j in range(NYL):
            for t in range(EXPERTS // PACK):
                tile = out[j * FEATS : (j + 1) * FEATS, t * 128 : (t + 1) * 128]
                for i in range(PACK):
                    packed = jnp.zeros((rows, 128), F32)
                    for q in range(PACK):
                        part = tile[q * rows : (q + 1) * rows, :]
                        shift = (q - i) % PACK * PIECE
                        part = pltpu.roll(part, shift, 1) if shift else part
                        packed = jnp.where(group == q, part, packed)
                    out_ref[t * PACK + i, j, to] = packed.astype(BF)


def combine_body(target_ref, gates_ref, in_ref, out_ref):
    rows = FEATS // PACK
    target = jnp.concatenate([target_ref[0:1, :], target_ref[1:2, :]], axis=1)
    slot = iota((128, 2 * ROW_DEV), 0) % PIECE
    group = iota((rows, 128), 1) // PIECE
    picked = jnp.zeros((FEATS, 2 * ROW_DEV), F32)
    for e in range(EXPERTS):
        for h in range(NC):
            place = one_hot(target - (e * CAP + h * PIECE) == slot)
            total = in_ref[e, 0, h].astype(F32)
            for j in range(1, NYL):
                total += in_ref[e, j, h].astype(F32)
            total = jnp.concatenate([jnp.where(group == q, total, 0.0) for q in range(PACK)], axis=0)
            hi = total.astype(BF)
            rest = (total - hi.astype(F32)).astype(BF)
            picked += dot(hi, place) + dot(rest, place)
    mixed = gates_ref[0:1, :] * picked[:, :ROW_DEV] + gates_ref[1:2, :] * picked[:, ROW_DEV:]
    out_ref[...] = mixed.astype(BF)


def cut_body(place_ref, in_ref, *out_refs):
    width = out_refs[0].shape[1]
    for m, out_ref in enumerate(out_refs):
        start = pl.multiple_of(place_ref[m] * width, width)
        out_ref[...] = in_ref[:, pl.ds(start, width)]


def join_body(place_ref, *refs):
    pieces, out_ref = refs[:NYL], refs[NYL]
    core = place_ref[NYL]
    for m, piece in enumerate(pieces):
        rows = pl.ds(pl.multiple_of(place_ref[m] * FEATS, FEATS), FEATS)
        for z in range(NZ):
            for k, at in enumerate((core, 1 - core)):
                cols = pl.ds(pl.multiple_of((2 * z + at) * 128, 128), 128)
                start = (2 * z + k) * 128
                out_ref[rows, start : start + 128] = piece[:, cols]


def per_device(hidden_state, norm_gain, routes, gates, w_gate, w_up, w_down):
    quarter = 2 * lax.axis_index("ya") + lax.axis_index("yb")
    core = lax.axis_index("c")
    swap = [(0, 1), (1, 0)]
    places = [quarter ^ m for m in range(NYL)] + [core, lax.axis_index("yb")]
    places = jnp.stack(places).astype(I32)

    outgoing, targets = call(
        dispatch_body,
        (
            jax.ShapeDtypeStruct((EXPERTS, NYA, NC, PIECE, ROW_DEV), BF),
            jax.ShapeDtypeStruct((8, ROW_DEV), I32),
        ),
        hidden_state.T,
        norm_gain[None, :],
        routes.T,
        limit=WHOLE_VMEM,
    )
    with jax.named_scope("rows_over_xyc"):
        incoming = lax.all_to_all(
            outgoing.reshape(EXPERTS * GROUP, PIECE, ROW_DEV),
            ("x", "yh", "ya", "c"),
            split_axis=0,
            concat_axis=0,
            tiled=True,
        )
    incoming = incoming.reshape(EXPERTS, GROUP, PIECE, ROW_DEV)
    block = call(
        turn_body,
        jax.ShapeDtypeStruct((NZ, DEPTH, 128), BF),
        incoming,
        scratch_shapes=[pltpu.VMEM((DEPTH, 128), BF)],
    )
    with jax.named_scope("features_over_z"):
        features = lax.all_to_all(block, "z", split_axis=0, concat_axis=0, tiled=True)

    split = (NYA, NYB, NZ, NC * FEATS, 128)
    half = jax.ShapeDtypeStruct((2, NYA, NZ, NC * FEATS, 128), BF)
    gate_cols, up_cols = w_gate[0].reshape(split), w_up[0].reshape(split)
    hbm = pl.BlockSpec(memory_space=pltpu.HBM)

    def half_of(own, gate_cols, up_cols):
        return pl.pallas_call(
            functools.partial(half_body, own),
            out_shape=half,
            in_specs=[pl.BlockSpec(memory_space=pltpu.SMEM), hbm, hbm],
            out_specs=hbm,
            scratch_shapes=[pltpu.VMEM(half.shape, BF), pltpu.SemaphoreType.DMA((4 * NYA,))],
            compiler_params=pltpu.CompilerParams(vmem_limit_bytes=WHOLE_VMEM),
            cost_estimate=pl.CostEstimate(flops=0, bytes_accessed=3_000_000, transcendentals=0),
        )(places, gate_cols, up_cols)

    w_sent = half_of(False, gate_cols, up_cols)
    with jax.named_scope("gate_up_over_y"):
        w_next = lax.ppermute(w_sent, "yb", swap)
    down = w_down[0]
    units = down.shape[0] // NYL
    piece = jax.ShapeDtypeStruct((FEATS, units), BF)
    pieces = list(call(cut_body, (piece,) * NYL, places, down.T, scalars=1))

    def over_y(m, after):
        sent, _ = lax.optimization_barrier((pieces[m], after))
        with jax.named_scope("down_over_y"):
            return lax.ppermute(sent, ("ya", "yb"), [(i, i ^ m) for i in range(NYL)])

    pieces[2] = over_y(2, block)
    w_own = half_of(True, gate_cols, up_cols)
    w_own, _ = lax.optimization_barrier((w_own, block))
    with jax.named_scope("gate_up_over_c"):
        w_core = lax.ppermute(w_own, "c", swap)
    w_next, pieces[2], w_core = lax.optimization_barrier((w_next, pieces[2], w_core))
    pieces[1] = over_y(1, w_next)
    with jax.named_scope("gate_up_over_c"):
        w_next_core = lax.ppermute(w_next, "c", swap)

    flops = 2 * SLOTS * D // 2 * 512
    sent = call(
        neighbour_body,
        jax.ShapeDtypeStruct((SLOTS + EXTRA, 512), BF),
        w_next,
        w_next_core,
        features,
        flops=flops,
        moved=5_000_000,
        scratch_shapes=[pltpu.VMEM((SLOTS, 512), F32)],
    )
    with jax.named_scope("hidden_over_y"):
        got = lax.ppermute(sent, "yb", swap)
    own, squares = call(
        own_body,
        (jax.ShapeDtypeStruct((SLOTS, 512), F32), jax.ShapeDtypeStruct((8, SLOTS), F32)),
        w_own,
        w_core,
        features,
        flops=flops,
        moved=5_000_000,
    )
    acts = call(act_body, jax.ShapeDtypeStruct((NZ, SLOTS, 256), BF), own, squares, got)
    with jax.named_scope("units_over_z"):
        acts = lax.all_to_all(acts, "z", split_axis=0, concat_axis=0, tiled=True)

    pieces[3] = over_y(3, own)
    part = jax.ShapeDtypeStruct((NYL * FEATS, units), BF)
    down_own = call(join_body, part, places, *pieces, scalars=1)
    with jax.named_scope("down_over_c"):
        down_other = lax.ppermute(down_own, "c", swap)

    rows = FEATS // PACK
    out = call(
        down_body,
        jax.ShapeDtypeStruct((EXPERTS, NYL, NC, rows, 128), BF),
        places,
        down_own,
        down_other,
        acts,
        scalars=1,
        flops=2 * NC * NYL * FEATS * units * SLOTS,
        moved=5_000_000,
    )
    with jax.named_scope("out_over_xyc"):
        back = lax.all_to_all(
            out.reshape(EXPERTS * NYL * NC, rows, 128),
            ("x", "yh", "ya", "yb", "c"),
            split_axis=0,
            concat_axis=0,
            tiled=True,
        )
    back = back.reshape(EXPERTS, NYL, NC, rows, 128)
    return call(
        combine_body, jax.ShapeDtypeStruct((FEATS, ROW_DEV), BF), targets, gates.T, back
    ).T


def solution(mesh):
    fine = Mesh(
        mesh.devices.reshape(NX, NYH, NYA, NYB, NZ, NC), ("x", "yh", "ya", "yb", "z", "c")
    )
    exp, tp = ("x", "yh"), ("ya", "yb", "z", "c")
    in_specs = (
        P(exp, tp),
        P(tp),
        P(exp, None),
        P(exp, None),
        P(exp, None, tp),
        P(exp, None, tp),
        P(exp, None, tp),
    )
    return jax.shard_map(
        per_device, mesh=fine, in_specs=in_specs, out_specs=P(exp, tp), check_vma=False
    )
```

```python
import functools

import jax
import jax.numpy as jnp
from jax import lax
from jax.experimental import pallas as pl
from jax.experimental.pallas import tpu as pltpu
from jax.sharding import Mesh, PartitionSpec as P

D = 6144
EXPERTS = 8
NX, NYH, NYA, NYB, NZ, NC = 4, 2, 2, 2, 8, 2
NYL = NYA * NYB
NZC = NZ * NC
FEATS = 96
GROUP = NYA * NC
ROW_DEV = 128
CAP = 64
PIECE = CAP // NC
SLOTS = EXPERTS * PIECE
EXTRA = 16
TILES = GROUP * FEATS // 128
PARTS = SLOTS // 128 * 8
DEPTH = TILES * SLOTS + PARTS
PACK = 128 // PIECE
BF = jnp.bfloat16
F32 = jnp.float32
I32 = jnp.int32
BIG = 3.0e38
NT = (((1,), (1,)), ((), ()))
WHOLE_VMEM = 62 * 1024 * 1024
VMEM_LIMIT = 40 * 1024 * 1024


def iota(shape, dim):
    return lax.broadcasted_iota(I32, shape, dim)


def one_hot(condition):
    return jnp.where(condition, 1.0, 0.0).astype(BF)


def dot(a, b, dims=(((1,), (0,)), ((), ()))):
    return lax.dot_general(a, b, dims, preferred_element_type=F32)


def call(body, out_shape, *args, flops=1_000_000, moved=1_000_000, scalars=0, after=(), limit=VMEM_LIMIT, **kw):
    specs = [pl.BlockSpec(memory_space=pltpu.SMEM)] * scalars
    specs += [pl.BlockSpec(memory_space=pltpu.VMEM)] * (len(args) - scalars)
    specs += [pl.BlockSpec(memory_space=pl.ANY)] * len(after)
    return pl.pallas_call(
        body,
        out_shape=out_shape,
        in_specs=specs,
        out_specs=jax.tree.map(lambda _: pl.BlockSpec(memory_space=pltpu.VMEM), out_shape),
        compiler_params=pltpu.CompilerParams(vmem_limit_bytes=limit),
        cost_estimate=pl.CostEstimate(flops=flops, bytes_accessed=moved, transcendentals=0),
        **kw,
    )(*args, *after)


def dispatch_body(hidden_ref, gain_ref, routes_ref, out_ref, target_ref):
    diagonal = iota((FEATS, FEATS), 0) == iota((FEATS, FEATS), 1)
    gain = jnp.sum(jnp.where(diagonal, gain_ref[...].astype(F32), 0.0), axis=1, keepdims=True)
    values = hidden_ref[...].astype(F32)
    scaled = jnp.clip(values * gain, -BIG, BIG)
    squares = jnp.minimum(jnp.sum(values * values, axis=0, keepdims=True), BIG)
    hi = squares.astype(BF).astype(F32)
    mid = (squares - hi).astype(BF).astype(F32)
    low = squares - hi - mid
    row = iota((ROW_DEV - FEATS, ROW_DEV), 0)
    parts = jnp.where(row == 0, hi, jnp.where(row == 1, mid, jnp.where(row == 2, low, 0.0)))
    rows = jnp.concatenate([scaled, parts], axis=0).astype(BF)

    first, second = routes_ref[0:1, :], routes_ref[1:2, :]
    expert = iota((2 * EXPERTS, ROW_DEV), 0)
    named0, named1 = expert == first, expert == second
    earlier = one_hot(iota((ROW_DEV, ROW_DEV), 0) < iota((ROW_DEV, ROW_DEV), 1))
    before = dot(one_hot(named0 | named1), earlier)
    rank0 = jnp.sum(jnp.where(named0, before, 0.0), axis=0, keepdims=True).astype(I32)
    rank1 = jnp.sum(jnp.where(named1, before, 0.0), axis=0, keepdims=True).astype(I32)
    target0, target1 = first * CAP + rank0, second * CAP + rank1
    target_ref[...] = jnp.where(iota((8, ROW_DEV), 0) == 0, target0, target1)
    slot = iota((EXPERTS * CAP, ROW_DEV), 0)
    place = one_hot((slot == target0) | (slot == target1))
    sent = dot(place, rows, NT).astype(BF).reshape(EXPERTS, NC, PIECE, ROW_DEV)
    for j in range(NYA):
        out_ref[:, j] = sent


def turn_body(in_ref, out_ref, turned_ref):
    row, lane = iota((EXTRA, ROW_DEV), 0), iota((EXTRA, ROW_DEV), 1)
    source, column = iota((ROW_DEV, ROW_DEV), 0), iota((ROW_DEV, ROW_DEV), 1)
    extra = jnp.zeros((EXTRA, SLOTS), F32)
    rows = [in_ref[:, j].reshape(SLOTS, ROW_DEV) for j in range(GROUP)]
    for t in range(TILES):
        tile = jnp.zeros((SLOTS, ROW_DEV), F32)
        for j in range(GROUP):
            shift = t * ROW_DEV - j * FEATS
            if -ROW_DEV < shift < FEATS:
                pick = one_hot((source - column == shift) & (source < FEATS))
                tile += dot(rows[j], pick)
        turned_ref[t * SLOTS : (t + 1) * SLOTS, :] = tile.astype(BF)
    for j in range(GROUP):
        pick = one_hot((row == lane - FEATS) & (row < 3))
        extra += dot(pick, rows[j], NT)
    squares = jnp.minimum(jnp.sum(extra, axis=0, keepdims=True), BIG)
    hi = squares.astype(BF).astype(F32)
    mid = (squares - hi).astype(BF).astype(F32)
    row = iota((8, SLOTS), 0)
    extra = jnp.where(row == 0, hi, jnp.where(row == 1, mid, squares - hi - mid))
    extra = jnp.where(row < 3, extra, 0.0)
    tiles = [extra[:, t * 128 : (t + 1) * 128] for t in range(SLOTS // 128)]
    turned_ref[TILES * SLOTS :, :] = jnp.concatenate(tiles, axis=0).astype(BF)
    for z in range(NZ):
        out_ref[z] = turned_ref[...]


def half_body(own, place_ref, gate_ref, up_ref, out_ref, held_ref, sem):
    parity = place_ref[NYL + 1] if own else 1 - place_ref[NYL + 1]
    parts = [(i, j, ref) for i, ref in enumerate((gate_ref, up_ref)) for j in range(NYA)]
    to_held, to_out = [], []
    for k, (i, j, ref) in enumerate(parts):
        to_held.append(pltpu.make_async_copy(ref.at[j, parity], held_ref.at[i, j], sem.at[k]))
        to_out.append(pltpu.make_async_copy(held_ref.at[i, j], out_ref.at[i, j], sem.at[len(parts) + k]))
        to_held[-1].start()
    for first, second in zip(to_held, to_out):
        first.wait()
        second.start()
    for second in to_out:
        second.wait()


def products(x_ref, weight_refs, acc_ref):
    for z in range(0, NZ, 2):
        tiles, columns = [], []
        for i in range(z, z + 2):
            tiles += [x_ref[i, t * SLOTS : (t + 1) * SLOTS, :] for t in range(TILES)]
            weights = [w[k, :, i].reshape(GROUP * FEATS, 128) for w in weight_refs for k in range(2)]
            columns.append(jnp.concatenate(weights, axis=1))
        total = dot(jnp.concatenate(tiles, axis=1), jnp.concatenate(columns, axis=0))
        if z == 0:
            acc_ref[...] = total
        else:
            acc_ref[...] += total


def sums_of_squares(x_ref):
    parts = jnp.zeros((PARTS, 128), F32)
    for z in range(NZ):
        parts += x_ref[z, TILES * SLOTS :, :].astype(F32)
    sums = [
        jnp.sum(parts[t * 8 : (t + 1) * 8], axis=0, keepdims=True) for t in range(SLOTS // 128)
    ]
    return jnp.concatenate(sums, axis=1)


def neighbour_body(w_ref, w2_ref, x_ref, out_ref, acc_ref):
    products(x_ref, (w_ref, w2_ref), acc_ref)
    out_ref[:SLOTS, :] = acc_ref[...].astype(BF)
    squares = jnp.minimum(sums_of_squares(x_ref), BIG)
    hi = squares.astype(BF).astype(F32)
    mid = (squares - hi).astype(BF).astype(F32)
    row = iota((EXTRA, SLOTS), 0)
    parts = jnp.where(row == 0, hi, jnp.where(row == 1, mid, squares - hi - mid))
    parts = jnp.where(row < 3, parts, 0.0).astype(BF)
    out_ref[SLOTS:, :] = jnp.concatenate([parts, parts], axis=1)


def own_body(w_ref, w2_ref, x_ref, out_ref, squares_ref):
    products(x_ref, (w_ref, w2_ref), out_ref)
    squares_ref[...] = jnp.broadcast_to(sums_of_squares(x_ref), (8, SLOTS))


def act_body(own_ref, squares_ref, got_ref, out_ref):
    diagonal = iota((128, 128), 0) == iota((128, 128), 1)
    got = jnp.sum(got_ref[SLOTS:, :SLOTS].astype(F32), axis=0, keepdims=True)
    squares = squares_ref[0:1, :] + got
    for t in range(SLOTS // 128):
        rows = slice(t * 128, (t + 1) * 128)
        column = jnp.sum(jnp.where(diagonal, squares[:, rows], 0.0), axis=1, keepdims=True)
        inv_rms = lax.rsqrt(column / D + 1e-05)
        hidden = (own_ref[rows, :] + got_ref[rows, :].astype(F32)) * inv_rms
        for k in range(NC):
            gate = hidden[:, 256 * k : 256 * k + 128]
            up = hidden[:, 256 * k + 128 : 256 * k + 256]
            act = (gate / (1.0 + jnp.exp(-gate)) * up).astype(BF)
            for z in range(NZ):
                out_ref[z, rows, 128 * k : 128 * (k + 1)] = act


def down_body(place_ref, own_ref, other_ref, x_ref, out_ref):
    rows = FEATS // PACK
    group = iota((rows, 128), 1) // PIECE
    core = place_ref[NYL]
    columns = own_ref.shape[0]
    total = jnp.zeros((2 * columns, SLOTS), F32)
    for z in range(NZ):
        cols = slice(z * 256, (z + 1) * 256)
        swapped = jnp.concatenate(
            [other_ref[:, z * 256 + 128 : (z + 1) * 256], other_ref[:, z * 256 : z * 256 + 128]], axis=1
        )
        total += dot(jnp.concatenate([own_ref[:, cols], swapped], axis=0), x_ref[z], NT)
    for k in range(NC):
        out = total[k * columns : (k + 1) * columns]
        to = core if k == 0 else 1 - core
        for j in range(NYL):
            for t in range(EXPERTS // PACK):
                tile = out[j * FEATS : (j + 1) * FEATS, t * 128 : (t + 1) * 128]
                for i in range(PACK):
                    packed = jnp.zeros((rows, 128), F32)
                    for q in range(PACK):
                        part = tile[q * rows : (q + 1) * rows, :]
                        shift = (q - i) % PACK * PIECE
                        part = pltpu.roll(part, shift, 1) if shift else part
                        packed = jnp.where(group == q, part, packed)
                    out_ref[t * PACK + i, j, to] = packed.astype(BF)


def combine_body(target_ref, gates_ref, in_ref, out_ref):
    rows = FEATS // PACK
    target = jnp.concatenate([target_ref[0:1, :], target_ref[1:2, :]], axis=1)
    slot = iota((128, 2 * ROW_DEV), 0) % PIECE
    group = iota((rows, 128), 1) // PIECE
    picked = jnp.zeros((FEATS, 2 * ROW_DEV), F32)
    for e in range(EXPERTS):
        places, totals = [], []
        for h in range(NC):
            places.append(one_hot(target - (e * CAP + h * PIECE) == slot))
            total = in_ref[e, 0, h].astype(F32)
            for j in range(1, NYL):
                total += in_ref[e, j, h].astype(F32)
            totals.append(
                jnp.concatenate([jnp.where(group == q, total, 0.0) for q in range(PACK)], axis=0)
            )
        total = jnp.concatenate(totals, axis=1)
        hi = total.astype(BF)
        rest = (total - hi.astype(F32)).astype(BF)
        both = dot(jnp.concatenate([hi, rest], axis=0), jnp.concatenate(places, axis=0))
        picked += both[:FEATS] + both[FEATS:]
    mixed = gates_ref[0:1, :] * picked[:, :ROW_DEV] + gates_ref[1:2, :] * picked[:, ROW_DEV:]
    out_ref[...] = mixed.astype(BF)


def cut_body(place_ref, in_ref, *out_refs):
    width = out_refs[0].shape[1]
    for m, out_ref in enumerate(out_refs):
        start = pl.multiple_of(place_ref[m] * width, width)
        out_ref[...] = in_ref[:, pl.ds(start, width)]


def join_body(place_ref, *refs):
    pieces, out_ref = refs[:NYL], refs[NYL]
    core = place_ref[NYL]
    for m, piece in enumerate(pieces):
        rows = pl.ds(pl.multiple_of(place_ref[m] * FEATS, FEATS), FEATS)
        for z in range(NZ):
            for k, at in enumerate((core, 1 - core)):
                cols = pl.ds(pl.multiple_of((2 * z + at) * 128, 128), 128)
                start = (2 * z + k) * 128
                out_ref[rows, start : start + 128] = piece[:, cols]


def per_device(hidden_state, norm_gain, routes, gates, w_gate, w_up, w_down):
    quarter = 2 * lax.axis_index("ya") + lax.axis_index("yb")
    core = lax.axis_index("c")
    swap = [(0, 1), (1, 0)]
    places = [quarter ^ m for m in range(NYL)] + [core, lax.axis_index("yb")]
    places = jnp.stack(places).astype(I32)

    outgoing, targets = call(
        dispatch_body,
        (
            jax.ShapeDtypeStruct((EXPERTS, NYA, NC, PIECE, ROW_DEV), BF),
            jax.ShapeDtypeStruct((8, ROW_DEV), I32),
        ),
        hidden_state.T,
        norm_gain[None, :],
        routes.T,
        limit=WHOLE_VMEM,
    )
    with jax.named_scope("rows_over_xyc"):
        incoming = lax.all_to_all(
            outgoing.reshape(EXPERTS * GROUP, PIECE, ROW_DEV),
            ("x", "yh", "ya", "c"),
            split_axis=0,
            concat_axis=0,
            tiled=True,
        )
    incoming = incoming.reshape(EXPERTS, GROUP, PIECE, ROW_DEV)
    block = call(
        turn_body,
        jax.ShapeDtypeStruct((NZ, DEPTH, 128), BF),
        incoming,
        scratch_shapes=[pltpu.VMEM((DEPTH, 128), BF)],
    )
    with jax.named_scope("features_over_z"):
        features = lax.all_to_all(block, "z", split_axis=0, concat_axis=0, tiled=True)

    split = (NYA, NYB, NZ, NC * FEATS, 128)
    half = jax.ShapeDtypeStruct((2, NYA, NZ, NC * FEATS, 128), BF)
    gate_cols, up_cols = w_gate[0].reshape(split), w_up[0].reshape(split)
    hbm = pl.BlockSpec(memory_space=pltpu.HBM)

    def half_of(own, gate_cols, up_cols):
        return pl.pallas_call(
            functools.partial(half_body, own),
            out_shape=half,
            in_specs=[pl.BlockSpec(memory_space=pltpu.SMEM), hbm, hbm],
            out_specs=hbm,
            scratch_shapes=[pltpu.VMEM(half.shape, BF), pltpu.SemaphoreType.DMA((4 * NYA,))],
            compiler_params=pltpu.CompilerParams(vmem_limit_bytes=WHOLE_VMEM),
            cost_estimate=pl.CostEstimate(flops=0, bytes_accessed=3_000_000, transcendentals=0),
        )(places, gate_cols, up_cols)

    w_sent = half_of(False, gate_cols, up_cols)
    with jax.named_scope("gate_up_over_y"):
        w_next = lax.ppermute(w_sent, "yb", swap)
    down = w_down[0]
    units = down.shape[0] // NYL
    piece = jax.ShapeDtypeStruct((FEATS, units), BF)
    pieces = list(call(cut_body, (piece,) * NYL, places, down.T, scalars=1))

    def over_y(m, after):
        sent, _ = lax.optimization_barrier((pieces[m], after))
        with jax.named_scope("down_over_y"):
            return lax.ppermute(sent, ("ya", "yb"), [(i, i ^ m) for i in range(NYL)])

    pieces[2] = over_y(2, block)
    w_own = half_of(True, gate_cols, up_cols)
    w_own, _ = lax.optimization_barrier((w_own, block))
    with jax.named_scope("gate_up_over_c"):
        w_core = lax.ppermute(w_own, "c", swap)
    w_next, pieces[2], w_core = lax.optimization_barrier((w_next, pieces[2], w_core))
    pieces[1] = over_y(1, w_next)
    with jax.named_scope("gate_up_over_c"):
        w_next_core = lax.ppermute(w_next, "c", swap)

    flops = 2 * SLOTS * D // 2 * 512
    sent = call(
        neighbour_body,
        jax.ShapeDtypeStruct((SLOTS + EXTRA, 512), BF),
        w_next,
        w_next_core,
        features,
        flops=flops,
        moved=5_000_000,
        scratch_shapes=[pltpu.VMEM((SLOTS, 512), F32)],
    )
    with jax.named_scope("hidden_over_y"):
        got = lax.ppermute(sent, "yb", swap)
    own, squares = call(
        own_body,
        (jax.ShapeDtypeStruct((SLOTS, 512), F32), jax.ShapeDtypeStruct((8, SLOTS), F32)),
        w_own,
        w_core,
        features,
        flops=flops,
        moved=5_000_000,
    )
    acts = call(act_body, jax.ShapeDtypeStruct((NZ, SLOTS, 256), BF), own, squares, got)
    with jax.named_scope("units_over_z"):
        acts = lax.all_to_all(acts, "z", split_axis=0, concat_axis=0, tiled=True)

    pieces[3] = over_y(3, own)
    part = jax.ShapeDtypeStruct((NYL * FEATS, units), BF)
    down_own = call(join_body, part, places, *pieces, scalars=1)
    with jax.named_scope("down_over_c"):
        down_other = lax.ppermute(down_own, "c", swap)

    rows = FEATS // PACK
    out = call(
        down_body,
        jax.ShapeDtypeStruct((EXPERTS, NYL, NC, rows, 128), BF),
        places,
        down_own,
        down_other,
        acts,
        scalars=1,
        flops=2 * NC * NYL * FEATS * units * SLOTS,
        moved=5_000_000,
    )
    with jax.named_scope("out_over_xyc"):
        back = lax.all_to_all(
            out.reshape(EXPERTS * NYL * NC, rows, 128),
            ("x", "yh", "ya", "yb", "c"),
            split_axis=0,
            concat_axis=0,
            tiled=True,
        )
    back = back.reshape(EXPERTS, NYL, NC, rows, 128)
    return call(
        combine_body, jax.ShapeDtypeStruct((FEATS, ROW_DEV), BF), targets, gates.T, back
    ).T


def solution(mesh):
    fine = Mesh(
        mesh.devices.reshape(NX, NYH, NYA, NYB, NZ, NC), ("x", "yh", "ya", "yb", "z", "c")
    )
    exp, tp = ("x", "yh"), ("ya", "yb", "z", "c")
    in_specs = (
        P(exp, tp),
        P(tp),
        P(exp, None),
        P(exp, None),
        P(exp, None, tp),
        P(exp, None, tp),
        P(exp, None, tp),
    )
    return jax.shard_map(
        per_device, mesh=fine, in_specs=in_specs, out_specs=P(exp, tp), check_vma=False
    )
```
